128 devices in a mesh: section: 8 (over y, core), shard: 16 (over x, z).
Axes of the slice: x: 4, y: 4, z: 4, core: 2. Of those that a mesh axis runs over, the one named last changes fastest.
Arguments:
- fresh_rows: bfloat16 [8, 16, 8, 64, 4096], P('section', 'shard'), may hold values from -0.09375 to 0.09375
- row_bounds: int32 [8, 129], replicated, may hold values from 0 to 6144, as said below
- layer_section: int32 [8], replicated, may hold values from 0 to 7, each once
- rows_in: bfloat16 [2, 16, 4096], replicated, may hold values from -6 to 6
- attn_norm: bfloat16 [8, 4096], P('section'), may hold values from 0.099609375 to 1.8984375
- q_proj: bfloat16 [8, 4096, 4096], P('section', None, 'shard'), may hold values from -0.09375 to 0.09375
- kv_proj: bfloat16 [8, 4096, 512], P('section', None, 'shard'), may hold values from -0.09375 to 0.09375
- o_proj: bfloat16 [8, 4096, 4096], P('section', 'shard'), may hold values from -0.09375 to 0.09375
- kv_cache: bfloat16 [8, 2, 16, 2, 2, 64, 128], P('section'), may hold values from -200 to 200
- cache_lengths: int32 [2, 16], replicated, may hold values from 1 to 64, 512 in all within a row
- moe_norm: bfloat16 [8, 4096], P('section'), may hold values from 0.099609375 to 1.8984375
- router: bfloat16 [8, 4096, 2], P('section'), may hold values from -13 to 13
- expert_ids: int32 [8, 2, 16], P('section'), may hold values from 0 to 1
Outputs:
- packed: bfloat16 [8, 16, 384, 4096], P('section', 'shard')
- block_scales: float32 [8, 16, 3, 32], P('section', 'shard')
- section_out: bfloat16 [8, 2, 16, 4096], P('section', None, 'shard')
The draws below stay inside these ranges and needn't reach their ends.
Inputs may be any that keep to these rules, and one draw needn't show every extreme that they name: row_bounds[l, 0] = 0 and row_bounds[l, 128] = 6144; every row_bounds[l, o] is within 8 of 48 * o, so an owner holds 32 to 64 rows of a layer, and in every layer some owner holds exactly 64. `cache_lengths`: the 16 rows of one micro-batch hold 512 cached positions in all, and in each micro-batch some row holds 64.
All inputs are finite; a program needn't handle non-finite values.
Results may differ from the reference program's by a relative error of at most 0.035.
Values may be sent and summed in bfloat16 or wider, within the bound.
No kernel may reach another device: no remote copies, remote signals or barrier semaphores. Data moves between devices by JAX's collectives and lax.ppermute only.
A program may use at most 128 MiB of HBM per device.

```python
import math
import jax
import jax.numpy as jnp
import numpy as np
from jax import lax

D = 4096
HD = 128
HEADS = 32
KVH = 2
EXPS = 2
QB = 128
EDGE = 8
MB = 2
ROWS = 16
CTX = 64
HPD = 128
ROWS_DEV = 384
PIECE = 48
CAPR = 64
LAYERS = 8
OWNERS = 128
LROWS = 6144
N_SECTION = 8
N_SHARD = 16


def draw_row_bounds(key, part):
    key = jax.random.fold_in(key, 7)
    drift_key, spot_key = jax.random.split(key)
    drift = jax.random.randint(drift_key, (LAYERS, OWNERS + 1), -EDGE, EDGE + 1)
    spot = jax.random.randint(spot_key, (LAYERS, 1), 1, OWNERS - 1)
    places = jnp.arange(OWNERS + 1, dtype=jnp.int32)[None, :]
    drift = jnp.where(places == spot, -EDGE, drift)
    drift = jnp.where(places == spot + 1, EDGE, drift)
    drift = jnp.where((places == 0) | (places == OWNERS), 0, drift)
    return (places * PIECE + drift).astype(jnp.int32)


def draw_kv_cache(key, part):
    key = jax.random.fold_in(key, 11)
    base_key = jax.random.fold_in(key, 0)
    value_key = jax.random.fold_in(key, 2)
    full_shape = (N_SECTION, MB, ROWS, 1, KVH, CTX, HD)
    cached_values = jnp.clip(jax.random.normal(value_key, full_shape, jnp.float32), -6.0, 6.0)
    cached_keys = jnp.clip(jax.random.normal(base_key, full_shape, jnp.float32), -6.0, 6.0)
    return jnp.concatenate((cached_keys, cached_values), axis=3).astype(jnp.bfloat16)


def draw_router(key, part):
    key = jax.random.fold_in(key, 13)
    column_key = jax.random.fold_in(key, 1)
    weights = jnp.clip(jax.random.normal(column_key, (N_SECTION, D, EXPS), jnp.float32), -6.0, 6.0) * D ** (-0.5)
    return weights.astype(jnp.bfloat16)


def set_ends(result, own_key, least, top_value):
    shape = result.shape
    index_at = [jax.random.randint(jax.random.fold_in(own_key, axis), (), 0, shape[axis]) for axis in range(len(shape))]
    result = result.at[tuple(index_at)].set(least)
    longest = shape.index(max(shape))
    index_at[longest] = (index_at[longest] + 1) % shape[longest]
    return result.at[tuple(index_at)].set(top_value)


def level_of(own_key, shape, shards, least, high):
    level, own = 1.0, jax.random.fold_in(own_key, 6)
    for dim, blocks in shards:
        steps = jnp.exp(jax.random.uniform(jax.random.fold_in(own, dim), (blocks,), jnp.float32, least / len(shards), high / len(shards)))
        level = level * jnp.repeat(steps, shape[dim] // blocks).reshape([-1 if axis == dim else 1 for axis in range(len(shape))])
    return level


def profile(number_of, total, bound, lean):
    weights = [(1 << 20) // math.isqrt(rank ** lean) + 1 for rank in range(2, number_of + 1)]
    spare, counts = total - bound - (number_of - 1), [1] * (number_of - 1)
    while spare > 0:
        free = [i for i in range(number_of - 1) if counts[i] < bound]
        whole, left = sum([weights[i] for i in free]), spare
        for i in free:
            more = min(bound - counts[i], max(1, left * weights[i] // whole), spare)
            counts[i] = counts[i] + more
            spare = spare - more
    return np.array([bound] + counts)


def uneven_parts(rng, amount, total, reach, slope):
    if amount == 2:
        one = jax.random.randint(rng, (), max(1, total - reach), min(reach, total - 1) + 1)
        return jnp.stack([one, total - one])
    tallies = jnp.asarray(profile(amount, total, reach, slope), jnp.int32)
    pairs = (amount - 1) // 2
    source_of, receiver = tallies[1:1 + 2 * pairs:2], tallies[2:2 + 2 * pairs:2]
    slack = jnp.minimum(source_of - 1, reach - receiver)
    passed = jax.random.randint(jax.random.fold_in(rng, 1), (pairs,), 0, 1 << 20) % (slack + 1)
    tallies = tallies.at[1:1 + 2 * pairs:2].set(source_of - passed).at[2:2 + 2 * pairs:2].set(receiver + passed)
    return tallies[jax.random.permutation(jax.random.fold_in(rng, 2), amount)]


def centred(stream_key, shape, spread, most, shards=(), kind=jnp.bfloat16):
    array = spread * jax.random.normal(stream_key, shape, jnp.float32)
    if shards:
        array = array * level_of(stream_key, shape, shards, -0.22, 0.18)
    return jnp.clip(array, -most, most).astype(kind)


def setup_inputs(seed: int = 0) -> dict:
    key_list = jax.random.split(jax.random.key(seed), 14)
    return {
        "fresh_rows": centred(key_list[0], (N_SECTION, N_SHARD, LAYERS, CAPR, D), D ** -0.5, 0.09375, ((0, 8), (1, 16))),
        "row_bounds": draw_row_bounds(jax.random.fold_in(key_list[13], 71), 0),
        "layer_section": jax.random.permutation(key_list[2], LAYERS).astype(jnp.int32),
        "rows_in": centred(key_list[3], (MB, ROWS, D), 1.0, 6.0),
        "attn_norm": jnp.clip(1.0 + 0.18 * jax.random.normal(key_list[4], (N_SECTION, D), jnp.float32), 0.099609375, 1.8984375).astype(jnp.bfloat16),
        "q_proj": centred(key_list[5], (N_SECTION, D, HEADS * HD), D ** -0.5, 0.09375, ((0, 8), (2, 16))),
        "kv_proj": centred(key_list[6], (N_SECTION, D, 2 * KVH * HD), D ** -0.5, 0.09375, ((0, 8), (2, 16))),
        "o_proj": centred(key_list[7], (N_SECTION, HEADS * HD, D), (HEADS * HD) ** -0.5, 0.09375, ((0, 8), (1, 16))),
        "kv_cache": draw_kv_cache(jax.random.fold_in(key_list[13], 71), 0),
        "cache_lengths": jax.vmap(lambda own: uneven_parts(own, ROWS, ROWS * CTX // 2, CTX, 2))(jax.random.split(key_list[9], MB)).reshape((MB, ROWS)).astype(jnp.int32),
        "moe_norm": jnp.clip(1.0 + 0.18 * jax.random.normal(key_list[10], (N_SECTION, D), jnp.float32), 0.099609375, 1.8984375).astype(jnp.bfloat16),
        "router": draw_router(jax.random.fold_in(key_list[13], 71), 0),
        "expert_ids": set_ends(jax.random.randint(key_list[12], (N_SECTION, MB, ROWS), 0, EXPS), jax.random.fold_in(key_list[12], 1), 0, EXPS - 1).astype(jnp.int32),
    }


CODE_LIMIT = 448.0
NORM_EPSILON = 1e-06

def widen(values):
    return lax.optimization_barrier(values).astype(jnp.float32)

def rms_scale(values, gain):
    wide = values.astype(jnp.float32)
    mean_sq = lax.optimization_barrier(jnp.mean(wide * wide, axis=-1, keepdims=True))
    return (wide * lax.rsqrt(mean_sq + NORM_EPSILON) * gain.astype(jnp.float32)).astype(jnp.bfloat16)

def block_quantize(rows):
    count_r, width = rows.shape
    tiles = rows.astype(jnp.float32).reshape(count_r // QB, QB, width // QB, QB)
    peak = lax.optimization_barrier(jnp.max(jnp.abs(tiles), axis=(1, 3)))
    scale = (peak + 1e-06) / CODE_LIMIT
    coded = (tiles / scale[:, None, :, None]).astype(jnp.bfloat16).reshape(count_r, width)
    return (coded, scale)

def dequant_in(normed, coded, scale):
    batch = normed.shape[0]
    units, width = coded.shape
    parts = jnp.einsum('bcj,uicj->buic', widen(normed).reshape(batch, width // QB, QB), widen(coded).reshape(units // QB, QB, width // QB, QB))
    return lax.optimization_barrier(jnp.sum(parts * scale[None, :, None, :], axis=3)).reshape(batch, units)

def dequant_out(hidden, coded, scale):
    batch = hidden.shape[0]
    units, width = coded.shape
    parts = jnp.einsum('bui,uicj->bucj', widen(hidden).reshape(batch, units // QB, QB), widen(coded).reshape(units // QB, QB, width // QB, QB))
    return lax.optimization_barrier(jnp.sum(parts * scale[None, :, :, None], axis=1)).reshape(batch, width)

def expert_term(normed, coded, scale):
    tiles_u = HPD // QB
    gate = dequant_in(normed, coded[:HPD], scale[:tiles_u])
    upper = dequant_in(normed, coded[HPD:2 * HPD], scale[tiles_u:2 * tiles_u])
    hidden = (jax.nn.silu(gate) * upper).astype(jnp.bfloat16)
    return dequant_out(hidden, coded[2 * HPD:], scale[2 * tiles_u:])

def attend(queries, keys, values, new_key, new_value, lengths):
    factor = HD ** (-0.5)
    scores = jnp.einsum('bhd,btd->bht', widen(queries), widen(keys)) * factor
    own_score = jnp.einsum('bhd,bd->bh', widen(queries), widen(new_key)) * factor
    live = jnp.arange(keys.shape[1], dtype=jnp.int32)[None, None, :] < lengths[:, None, None]
    scores = jnp.where(live, scores, -1e+30)
    peak = jnp.maximum(lax.optimization_barrier(jnp.max(scores, axis=2)), own_score)
    weights = jnp.where(live, jnp.exp(scores - peak[..., None]), 0.0)
    own = jnp.exp(own_score - peak)
    total = lax.optimization_barrier(jnp.sum(weights, axis=2)) + own
    weights = (weights / total[..., None]).astype(jnp.bfloat16)
    own = (own / total).astype(jnp.bfloat16)
    mixed = jnp.einsum('bht,btd->bhd', widen(weights), widen(values))
    mixed = mixed + widen(own)[..., None] * widen(new_value)[:, None, :]
    return mixed.astype(jnp.bfloat16)

def run_layer(state, section, micro, coded, scale, attn_norm, q_proj, kv_proj, o_proj, kv_cache, cache_lengths, moe_norm, router, expert_ids):
    group = HEADS // KVH
    normed = rms_scale(state, attn_norm[section])
    queries = jnp.dot(normed, q_proj[section], preferred_element_type=jnp.float32).astype(jnp.bfloat16)
    queries = queries.reshape(ROWS, HEADS, HD)
    fresh_kv = jnp.dot(normed, kv_proj[section], preferred_element_type=jnp.float32).astype(jnp.bfloat16)
    lengths = cache_lengths[micro]
    pieces = []
    for shared_head in range(KVH):
        new_key = fresh_kv[:, shared_head * HD:(shared_head + 1) * HD]
        new_value = fresh_kv[:, (KVH + shared_head) * HD:(KVH + shared_head + 1) * HD]
        pieces.append(attend(queries[:, shared_head * group:(shared_head + 1) * group], kv_cache[section, micro, :, 0, shared_head], kv_cache[section, micro, :, 1, shared_head], new_key, new_value, lengths))
    mixed = jnp.concatenate(pieces, axis=1).reshape(ROWS, HEADS * HD)
    residual = state.astype(jnp.float32) + jnp.dot(mixed, o_proj[section], preferred_element_type=jnp.float32)
    expert_input = rms_scale(residual, moe_norm[section])
    logits = jnp.dot(expert_input, router[section], preferred_element_type=jnp.float32)
    route_probs = jax.nn.softmax(logits, axis=-1)
    chosen = expert_ids[section, micro]
    picked = chosen[:, None] == jnp.arange(EXPS, dtype=jnp.int32)[None, :]
    route_weight = lax.optimization_barrier(jnp.sum(jnp.where(picked, route_probs, 0.0), axis=1))
    total = jnp.zeros((ROWS, D), jnp.float32)
    for part in range(N_SHARD):
        expert = part // (N_SHARD // EXPS)
        mine = route_weight * (chosen == expert).astype(jnp.float32)
        total = total + expert_term(expert_input, coded[part], scale[part]) * mine[:, None]
    return (residual + total).astype(jnp.bfloat16)

def reference(fresh_rows, row_bounds, layer_section, rows_in, attn_norm, q_proj, kv_proj, o_proj, kv_cache, cache_lengths, moe_norm, router, expert_ids):
    layer_ids = jnp.arange(LAYERS, dtype=jnp.int32)
    order = lax.optimization_barrier(jnp.sum(jnp.where(layer_section[None, :] == layer_ids[:, None], layer_ids[None, :], 0), axis=1)).astype(jnp.int32)
    flat = fresh_rows.reshape(OWNERS, LAYERS, CAPR, D)
    stream_pos = jnp.arange(LROWS, dtype=jnp.int32)
    coded_all = []
    scale_all = []
    for section in range(N_SECTION):
        layer = order[section]
        bounds = row_bounds[layer]
        owner = lax.optimization_barrier(jnp.sum((bounds[None, 1:OWNERS] <= stream_pos[:, None]).astype(jnp.int32), axis=1)).astype(jnp.int32)
        inner = (stream_pos - jnp.take(bounds, owner)).astype(jnp.int32)
        source = jnp.take(flat, layer, axis=1).reshape(OWNERS * CAPR, D)
        stream = jnp.take(source, owner * CAPR + inner, axis=0)
        dest = stream.reshape(N_SECTION, N_SHARD, PIECE, D).transpose(1, 0, 2, 3).reshape(N_SHARD, ROWS_DEV, D)
        coded, scale = jax.vmap(block_quantize)(dest)
        coded_all.append(coded)
        scale_all.append(scale)
    outputs = []
    for micro in range(MB):
        state = rows_in[micro]
        per_section = []
        for section in range(N_SECTION):
            state = run_layer(state, section, micro, coded_all[section], scale_all[section], attn_norm, q_proj, kv_proj, o_proj, kv_cache, cache_lengths, moe_norm, router, expert_ids)
            per_section.append(state)
        outputs.append(jnp.stack(per_section, axis=0))
    section_out = jnp.stack(outputs, axis=1)
    return (jnp.stack(coded_all, axis=0), jnp.stack(scale_all, axis=0), section_out)
```

```python
import jax
import jax.numpy as jnp
from jax import lax
from jax.experimental import pallas as pl
from jax.experimental.pallas import tpu as pltpu
from jax.sharding import PartitionSpec as P

HD = 128
HEADS = 32
KVH = 2
EXPS = 2
QB = 128
EDGE = 8
PIECE = 48
CODE_LIMIT = 448.0
NORM_EPSILON = 1e-06
MIB = 1024 * 1024

bf16 = jnp.bfloat16
f32 = jnp.float32
NT = (((1,), (1,)), ((), ()))


def pairs_of(move):
    result = []
    for s in range(8):
        for x in range(4):
            for z in range(4):
                s2, x2, z2 = move(s, x, z)
                result.append((s * 16 + x * 4 + z, s2 % 8 * 16 + x2 % 4 * 4 + z2 % 4))
    return result


AXES = ("section", "shard")


def send(value, move):
    return lax.ppermute(value, AXES, pairs_of(move))


def share_kernel(order, starts, ends, base, piece_ref, left_ref, right_ref, out_ref):
    d = pl.program_id(0)
    layer = order[d]
    first = starts[layer] - base[0]
    stop = ends[layer] - base[0]
    t = lax.broadcasted_iota(jnp.int32, (PIECE, 64), 0)
    r = lax.broadcasted_iota(jnp.int32, (PIECE, 64), 1)
    own = jnp.where((r == t - first) & (t < stop), 1.0, 0.0).astype(bf16)
    t = lax.broadcasted_iota(jnp.int32, (PIECE, 16), 0)
    r = lax.broadcasted_iota(jnp.int32, (PIECE, 16), 1)
    near = (r < 8) & (r == t) & (t < first)
    far = (r >= 8) & (r - 8 == t - stop) & (t >= stop)
    rim = jnp.where(near | far, 1.0, 0.0).astype(bf16)
    rims = jnp.concatenate((left_ref[0].astype(f32), right_ref[0].astype(f32)), axis=0).astype(bf16)
    total = jnp.dot(own, piece_ref[0], preferred_element_type=f32)
    total = total + jnp.dot(rim, rims, preferred_element_type=f32)
    out_ref[0] = total.astype(bf16)


def build_shares(order, starts, ends, base, pieces, from_left, from_right):
    layers, slots, width = pieces.shape
    return pl.pallas_call(
        share_kernel,
        grid_spec=pltpu.PrefetchScalarGridSpec(
            num_scalar_prefetch=4,
            grid=(layers,),
            in_specs=[
                pl.BlockSpec((1, slots, width), lambda d, o, *_: (o[d], 0, 0)),
                pl.BlockSpec((1, EDGE, width), lambda d, o, *_: (o[d], 0, 0)),
                pl.BlockSpec((1, EDGE, width), lambda d, o, *_: (o[d], 0, 0)),
            ],
            out_specs=pl.BlockSpec((1, PIECE, width), lambda d, *_: (d, 0, 0)),
        ),
        out_shape=jax.ShapeDtypeStruct((layers, PIECE, width), bf16),
        compiler_params=pltpu.CompilerParams(vmem_limit_bytes=24 * MIB),
        name="build_shares",
    )(order, starts, ends, base, pieces, from_left, from_right)


def quantize_kernel(rows_ref, coded_ref, scale_ref):
    step = pl.program_id(0)
    rows, width = rows_ref.shape
    cols = width // QB
    at_r = lax.broadcasted_iota(jnp.int32, scale_ref.shape, 0)
    at_c = lax.broadcasted_iota(jnp.int32, scale_ref.shape, 1)
    scales = jnp.where(step == 0, jnp.zeros(scale_ref.shape, f32), scale_ref[...])
    for i in range(rows // QB):
        for c in range(cols):
            tile = rows_ref[i * QB : (i + 1) * QB, c * QB : (c + 1) * QB].astype(f32)
            peak = jnp.max(jnp.max(jnp.abs(tile), axis=0, keepdims=True), axis=1, keepdims=True)
            scale = (peak + 1e-06) / CODE_LIMIT
            coded_ref[i * QB : (i + 1) * QB, c * QB : (c + 1) * QB] = (tile * (1.0 / scale)).astype(bf16)
            scales = jnp.where((at_r == i) & (at_c == step * cols + c), scale, scales)
    scale_ref[...] = scales


def quantize(rows):
    count, width = rows.shape
    chunk = 1024
    return pl.pallas_call(
        quantize_kernel,
        grid=(width // chunk,),
        in_specs=[pl.BlockSpec((count, chunk), lambda i: (0, i))],
        out_specs=[
            pl.BlockSpec((count, chunk), lambda i: (0, i)),
            pl.BlockSpec((count // QB, width // QB), lambda i: (0, 0)),
        ],
        out_shape=[
            jax.ShapeDtypeStruct((count, width), bf16),
            jax.ShapeDtypeStruct((count // QB, width // QB), f32),
        ],
        compiler_params=pltpu.CompilerParams(vmem_limit_bytes=24 * MIB),
        name="quantize",
    )(rows)


def rms(wide, gain):
    mean_sq = jnp.mean(wide * wide, axis=-1, keepdims=True)
    return (wide * lax.rsqrt(mean_sq + NORM_EPSILON) * gain.astype(f32)).astype(bf16)


def attention_kernel(tick, flags, place, *refs):
    (parts, gain, bounds, wq, wkv, wo, cache) = (refs[:4],) + refs[4:10]
    state, out, keep = refs[10:13]
    vq, vkv, vo, vk, vv, sems = refs[13:]

    @pl.when(flags[tick] == 1)
    def _():
        head = place[0]
        row = place[1]
        copies = [
            pltpu.make_async_copy(wq, vq, sems.at[0]),
            pltpu.make_async_copy(wkv.at[pl.ds(head * 4, 4)], vkv.at[pl.ds(0, 4)], sems.at[1]),
            pltpu.make_async_copy(wkv.at[pl.ds(8 + head * 4, 4)], vkv.at[pl.ds(4, 4)], sems.at[2]),
            pltpu.make_async_copy(cache.at[:, :, 0, head], vk, sems.at[3]),
            pltpu.make_async_copy(cache.at[:, :, 1, head], vv, sems.at[4]),
            pltpu.make_async_copy(wo, vo, sems.at[5]),
        ]
        for copy in copies:
            copy.start()
        total = parts[0][...].astype(f32)
        for part in parts[1:]:
            total = total + part[...].astype(f32)
        rounded = total.astype(bf16)
        state[...] = rounded
        rows = rounded.shape[0]
        wide = rounded.astype(f32)
        pick = lax.broadcasted_iota(jnp.int32, (rows, 1), 0)
        for micro in range(2):
            chosen = jnp.where(pick == micro * 16 + row, wide, 0.0)
            keep[micro : micro + 1, :] = jnp.sum(chosen, axis=0, keepdims=True)
        normed = rms(wide, gain[...])
        copies[0].wait()
        q = jnp.dot(normed, vq[...], preferred_element_type=f32).astype(bf16)
        copies[1].wait()
        copies[2].wait()
        pair = lax.dot_general(normed, vkv[...].reshape(2 * HD, -1), NT, preferred_element_type=f32)
        pair = pair.astype(bf16)
        q2 = jnp.concatenate((q[:, :HD], q[:, HD:]), axis=0)
        new_key = jnp.concatenate((pair[:, :HD], pair[:, :HD]), axis=0)
        new_value = jnp.concatenate((pair[:, HD:], pair[:, HD:]), axis=0).astype(f32)
        factor = HD ** (-0.5)
        own_score = jnp.sum(q2.astype(f32) * new_key.astype(f32), axis=-1, keepdims=True) * factor
        copies[3].wait()
        scores = lax.dot_general(q2, vk[...].reshape(-1, HD), NT, preferred_element_type=f32) * factor
        at = lax.broadcasted_iota(jnp.int32, scores.shape, 1)
        live = (at >= bounds[:, 0:1]) & (at < bounds[:, 1:2])
        scores = jnp.where(live, scores, -1e30)
        peak = jnp.maximum(jnp.max(scores, axis=-1, keepdims=True), own_score)
        weights = jnp.where(live, jnp.exp(scores - peak), 0.0)
        own = jnp.exp(own_score - peak)
        whole = jnp.sum(weights, axis=-1, keepdims=True) + own
        weights = (weights / whole).astype(bf16)
        own = (own / whole).astype(bf16).astype(f32)
        copies[4].wait()
        mixed = jnp.dot(weights, vv[...].reshape(-1, HD), preferred_element_type=f32)
        mixed = (mixed + own * new_value).astype(bf16)
        mixed = jnp.concatenate((mixed[:rows], mixed[rows:]), axis=1)
        copies[5].wait()
        out[...] = jnp.dot(mixed, vo[...], preferred_element_type=f32).astype(bf16)


def any_spec():
    return pl.BlockSpec(memory_space=pl.ANY)


def smem_spec():
    return pl.BlockSpec(memory_space=pltpu.SMEM)


def vmem_spec():
    return pl.BlockSpec(memory_space=pltpu.VMEM)


def attention(tick, flags, place, parts, gain, bounds, wq, wkv, wo, cache):
    rows, width = parts[0].shape
    mine = wq.shape[1]
    micro, batch, _, _, ctx, hd = cache.shape
    return pl.pallas_call(
        lambda *refs: attention_kernel(tick, *refs),
        in_specs=[smem_spec(), smem_spec()]
        + [vmem_spec()] * 6
        + [any_spec()] * 4,
        out_specs=[vmem_spec(), vmem_spec(), vmem_spec()],
        out_shape=[
            jax.ShapeDtypeStruct((rows, width), bf16),
            jax.ShapeDtypeStruct((rows, width), bf16),
            jax.ShapeDtypeStruct((2, width), f32),
        ],
        scratch_shapes=[
            pltpu.VMEM(wq.shape, bf16),
            pltpu.VMEM((8, 2 * HD // 8, width), bf16),
            pltpu.VMEM(wo.shape, bf16),
            pltpu.VMEM((micro, batch, ctx, hd), bf16),
            pltpu.VMEM((micro, batch, ctx, hd), bf16),
            pltpu.SemaphoreType.DMA((6,)),
        ],
        compiler_params=pltpu.CompilerParams(vmem_limit_bytes=28 * MIB),
        name="attention",
    )(flags, place, *parts, gain, bounds, wq, wkv, wo, cache)


def expert_kernel(tick, flags, place, *refs):
    state, parts, gain, router, chosen, rows_ref, out, vw, sems = (
        refs[0],
        refs[1:5],
    ) + refs[5:]

    @pl.when(flags[tick] == 1)
    def _():
        units = vw.shape[0] // 3
        copies = [
            pltpu.make_async_copy(rows_ref.at[pl.ds(0, 2 * units)], vw.at[pl.ds(0, 2 * units)], sems.at[0]),
            pltpu.make_async_copy(rows_ref.at[pl.ds(2 * units, units)], vw.at[pl.ds(2 * units, units)], sems.at[1]),
        ]
        for copy in copies:
            copy.start()
        total = parts[0][...].astype(f32)
        for part in parts[1:]:
            total = total + part[...].astype(f32)
        residual = state[...].astype(f32) + total
        entry = rms(residual, gain[...])
        wide = entry.astype(f32)
        first = jnp.sum(wide * router[0:1, :].astype(f32), axis=-1, keepdims=True)
        second = jnp.sum(wide * router[1:2, :].astype(f32), axis=-1, keepdims=True)
        peak = jnp.maximum(first, second)
        first = jnp.exp(first - peak)
        second = jnp.exp(second - peak)
        expert = place[2]
        prob = jnp.where(expert == 0, first, second) / (first + second)
        mine = jnp.where(chosen[...] == expert, prob, 0.0)
        copies[0].wait()
        both = lax.dot_general(entry, vw[0 : 2 * units, :], NT, preferred_element_type=f32)
        gate = both[:, :units]
        hidden = (gate * jax.nn.sigmoid(gate) * both[:, units:]).astype(bf16)
        copies[1].wait()
        down = jnp.dot(hidden, vw[2 * units :, :], preferred_element_type=f32)
        once = jnp.where(place[3] == 0, 1.0, 0.0)
        out[...] = (down * mine + residual * once).astype(bf16)


def experts(tick, flags, place, state, parts, gain, router, chosen, rows):
    return pl.pallas_call(
        lambda *refs: expert_kernel(tick, *refs),
        in_specs=[smem_spec(), smem_spec()] + [vmem_spec()] * 8 + [any_spec()],
        out_specs=vmem_spec(),
        out_shape=jax.ShapeDtypeStruct(state.shape, bf16),
        scratch_shapes=[pltpu.VMEM(rows.shape, bf16), pltpu.SemaphoreType.DMA((2,))],
        compiler_params=pltpu.CompilerParams(vmem_limit_bytes=28 * MIB),
        name="experts",
    )(flags, place, state, *parts, gain, router, chosen, rows)


def sum_parts(parts):
    total = parts[0].astype(f32)
    for part in parts[1:]:
        total = total + part.astype(f32)
    return total


def local(
    fresh_rows,
    row_bounds,
    layer_section,
    rows_in,
    attn_norm,
    q_proj,
    kv_proj,
    o_proj,
    kv_cache,
    cache_lengths,
    moe_norm,
    router,
    expert_ids,
):
    sections = lax.axis_size("section")
    shards = lax.axis_size("shard")
    section_pos = lax.axis_index("section")
    shard_pos = lax.axis_index("shard")
    width = rows_in.shape[2]

    pieces = fresh_rows[0, 0]
    layer_ids = jnp.arange(layer_section.shape[0], dtype=jnp.int32)
    order = jnp.sum(
        jnp.where(layer_section[None, :] == layer_ids[:, None], layer_ids[None, :], 0), axis=1
    ).astype(jnp.int32)
    owner = section_pos * shards + shard_pos
    base = (PIECE * owner).astype(jnp.int32)
    starts = lax.dynamic_slice_in_dim(row_bounds, owner, 1, 1)[:, 0]
    ends = lax.dynamic_slice_in_dim(row_bounds, owner + 1, 1, 1)[:, 0]
    slot = jnp.arange(pieces.shape[1], dtype=jnp.int32)[None, None, :]
    edge = jnp.arange(EDGE, dtype=jnp.int32)[None, :, None]
    pick = (slot == edge + (base + PIECE - starts)[:, None, None]).astype(bf16)
    to_right = jnp.einsum("lts,lsd->ltd", pick, pieces, preferred_element_type=f32).astype(bf16)
    to_left = pieces[:, :EDGE]
    count = sections * shards
    from_left = lax.ppermute(to_right, AXES, [(i, (i + 1) % count) for i in range(count)])
    from_right = lax.ppermute(to_left, AXES, [((i + 1) % count, i) for i in range(count)])
    shares = build_shares(order, starts, ends, base[None], pieces, from_left, from_right)
    arrived = lax.all_to_all(shares, "section", split_axis=0, concat_axis=0, tiled=True)
    dest_rows = arrived.reshape(sections * PIECE, width)
    coded, scale = quantize(dest_rows)

    micro, batch, _ = rows_in.shape
    rows = micro * batch
    flags = (layer_ids == section_pos).astype(jnp.int32)
    heads_dev = q_proj.shape[2] // HD
    shared_head = shard_pos * heads_dev // (HEADS // KVH)
    expert_pos = shard_pos // (shards // EXPS)
    place = jnp.stack([shared_head, shard_pos, expert_pos, shard_pos]).astype(jnp.int32)
    pair_weight = lax.all_gather(kv_proj[0].T, "shard", axis=0)
    low = jnp.arange(rows, dtype=jnp.int32) * kv_cache.shape[5]
    high = low + cache_lengths.reshape(rows)
    bounds = jnp.tile(jnp.stack((low, high), axis=1), (heads_dev, 1))
    router_rows = router[0].T
    chosen = expert_ids[0].reshape(rows, 1)

    entry = rows_in.reshape(rows, width)
    parts = (entry, jnp.zeros_like(entry), jnp.zeros_like(entry), jnp.zeros_like(entry))
    keep = jnp.zeros((micro, width), f32)
    for tick in range(sections):
        state, term, keep_new = attention(
            tick, flags, place, parts, attn_norm, bounds, q_proj[0], pair_weight, o_proj[0], kv_cache[0]
        )
        keep = jnp.where(flags[tick] == 1, keep_new, keep)
        summed = sum_parts(
            [term] + [send(term, lambda s, x, z, k=k: (s, x, z + k)) for k in (2, 1, 3)]
        ).astype(bf16)
        around = [summed] + [send(summed, lambda s, x, z, k=k: (s, x + k, z)) for k in (2, 1, 3)]
        term = experts(tick, flags, place, state, around, moe_norm, router_rows, chosen, dest_rows)
        summed = sum_parts(
            [term] + [send(term, lambda s, x, z, k=k: (s, x, z + k)) for k in (2, 1, 3)]
        ).astype(bf16)
        parts = [send(summed, lambda s, x, z, k=k: (s + 1, x + k, z)) for k in (2, 0, 1, 3)]
    final = sum_parts(parts)
    final = jnp.stack([lax.dynamic_index_in_dim(final, m * batch + shard_pos, 0, keepdims=False) for m in range(micro)])
    keep = jnp.where(section_pos == 0, final, keep).astype(bf16)
    outputs = send(keep, lambda s, x, z: (s - 1, x, z))
    return (coded[None, None], scale[None, None], outputs[None, :, None])


def solution(mesh):
    return jax.shard_map(
        local,
        mesh=mesh,
        in_specs=(
            P("section", "shard", None, None, None),
            P(),
            P(),
            P(),
            P("section", None),
            P("section", None, "shard"),
            P("section", None, "shard"),
            P("section", "shard", None),
            P("section", None, None, None, None, None, None),
            P(),
            P("section", None),
            P("section", None, None),
            P("section", None, None),
        ),
        out_specs=(
            P("section", "shard", None, None),
            P("section", "shard", None, None),
            P("section", None, "shard", None),
        ),
        check_vma=False,
    )
```

```python
import jax
import jax.numpy as jnp
from jax import lax
from jax.experimental import pallas as pl
from jax.experimental.pallas import tpu as pltpu
from jax.sharding import PartitionSpec as P

HD = 128
HEADS = 32
KVH = 2
EXPS = 2
QB = 128
EDGE = 8
PIECE = 48
CODE_LIMIT = 448.0
NORM_EPSILON = 1e-06
MIB = 1024 * 1024
RING_ATTENTION = (4, 5, 6, 7)
RING_EXPERTS = (3, 5, 6, 7)

bf16 = jnp.bfloat16
f32 = jnp.float32
NT = (((1,), (1,)), ((), ()))


def pairs_of(move):
    result = []
    for s in range(8):
        for x in range(4):
            for z in range(4):
                s2, x2, z2 = move(s, x, z)
                result.append((s * 16 + x * 4 + z, s2 % 8 * 16 + x2 % 4 * 4 + z2 % 4))
    return result


AXES = ("section", "shard")


def send(value, move):
    return lax.ppermute(value, AXES, pairs_of(move))


def share_kernel(order, starts, ends, base, piece_ref, left_ref, right_ref, out_ref):
    layer = order[pl.program_id(0)]
    first = starts[layer] - base[0]
    stop = ends[layer] - base[0]
    t = lax.broadcasted_iota(jnp.int32, (PIECE, 64), 0)
    r = lax.broadcasted_iota(jnp.int32, (PIECE, 64), 1)
    own = jnp.where((r == t - first) & (t < stop), 1.0, 0.0).astype(bf16)
    t = lax.broadcasted_iota(jnp.int32, (PIECE, 16), 0)
    r = lax.broadcasted_iota(jnp.int32, (PIECE, 16), 1)
    near = (r < EDGE) & (r == t) & (t < first)
    far = (r >= EDGE) & (r - EDGE == t - stop) & (t >= stop)
    rim = jnp.where(near | far, 1.0, 0.0).astype(bf16)

    rims = jnp.concatenate((left_ref[0].astype(f32), right_ref[0].astype(f32)), axis=0).astype(bf16)
    total = jnp.dot(own, piece_ref[0], preferred_element_type=f32)
    total = total + jnp.dot(rim, rims, preferred_element_type=f32)
    out_ref[0] = total.astype(bf16)


def build_shares(order, starts, ends, base, pieces, from_left, from_right):
    layers, slots, width = pieces.shape
    return pl.pallas_call(
        share_kernel,
        grid_spec=pltpu.PrefetchScalarGridSpec(
            num_scalar_prefetch=4,
            grid=(layers,),
            in_specs=[
                pl.BlockSpec((1, slots, width), lambda d, o, *_: (o[d], 0, 0)),
                pl.BlockSpec((1, EDGE, width), lambda d, o, *_: (o[d], 0, 0)),
                pl.BlockSpec((1, EDGE, width), lambda d, o, *_: (o[d], 0, 0)),
            ],
            out_specs=pl.BlockSpec((1, PIECE, width), lambda d, *_: (d, 0, 0)),
        ),
        out_shape=jax.ShapeDtypeStruct((layers, PIECE, width), bf16),
        compiler_params=pltpu.CompilerParams(vmem_limit_bytes=24 * MIB),
        name="build_shares",
    )(order, starts, ends, base, pieces, from_left, from_right)


def quantize_kernel(rows_ref, coded_ref, scale_ref):
    step = pl.program_id(0)
    rows, width = rows_ref.shape
    cols = width // QB
    at_r = lax.broadcasted_iota(jnp.int32, scale_ref.shape, 0)
    at_c = lax.broadcasted_iota(jnp.int32, scale_ref.shape, 1)
    scales = jnp.where(step == 0, jnp.zeros(scale_ref.shape, f32), scale_ref[...])

    for c in range(cols):
        at = slice(c * QB, (c + 1) * QB)
        for i in range(rows // QB):
            tile = rows_ref[i * QB : (i + 1) * QB, at].astype(f32)
            peak = jnp.max(jnp.max(jnp.abs(tile), axis=0, keepdims=True), axis=1, keepdims=True)
            scale = (peak + 1e-06) / CODE_LIMIT
            coded_ref[i * QB : (i + 1) * QB, at] = (tile * (1.0 / scale)).astype(bf16)
            scales = jnp.where((at_r == i) & (at_c == step * cols + c), scale, scales)
    scale_ref[...] = scales


def quantize(rows):
    count, width = rows.shape
    chunk = 1024
    return pl.pallas_call(
        quantize_kernel,
        grid=(width // chunk,),
        in_specs=[pl.BlockSpec((count, chunk), lambda i: (0, i))],
        out_specs=[
            pl.BlockSpec((count, chunk), lambda i: (0, i)),
            pl.BlockSpec((count // QB, width // QB), lambda i: (0, 0)),
        ],
        out_shape=[
            jax.ShapeDtypeStruct((count, width), bf16),
            jax.ShapeDtypeStruct((count // QB, width // QB), f32),
        ],
        compiler_params=pltpu.CompilerParams(vmem_limit_bytes=24 * MIB),
        name="quantize",
    )(rows)


CHUNK = 2048


def rows_at(refs, c):
    at = pl.ds(pl.multiple_of(c * CHUNK, CHUNK), CHUNK)
    return jnp.concatenate([ref[:, at].astype(f32) for ref in refs], axis=0)


def columns(c):
    return pl.ds(pl.multiple_of(c * CHUNK, CHUNK), CHUNK)


def inverse_rms(load, rows, width):
    def add(c, total):
        wide = load(c)
        return total + wide * wide

    total = lax.fori_loop(0, width // CHUNK, add, jnp.zeros((rows, CHUNK), f32))
    return lax.rsqrt(jnp.sum(total, axis=-1, keepdims=True) / width + NORM_EPSILON)


def any_spec():
    return pl.BlockSpec(memory_space=pltpu.HBM)


def smem_spec():
    return pl.BlockSpec(memory_space=pltpu.SMEM)


def vmem_spec():
    return pl.BlockSpec(memory_space=pltpu.VMEM)


SPLIT = 4


def piece_copies(pieces, target, sems, first):
    copies, at = [], 0
    parts = SPLIT // len(pieces)
    for i, piece in enumerate(pieces):
        size = piece.shape[0] // parts
        for j in range(parts):
            copies.append(
                pltpu.make_async_copy(
                    piece.at[pl.ds(j * size, size)],
                    target.at[pl.ds(at, size)],
                    sems.at[first * SPLIT + i * parts + j],
                )
            )
            at += size
    return copies


class Taker:
    def __init__(self, refs):
        self.refs = list(refs)

    def __call__(self, count):
        result = self.refs[:count]
        del self.refs[:count]
        return result


def lay_out(lists):
    return [x for pieces in lists for x in pieces], [len(pieces) for pieces in lists]


def project_kernel(place, *refs):
    take = Taker(refs)
    parts = take(4)
    gain, wq, wkv, q, pair, vq, sem = take(7)
    del place
    copies = piece_copies([wq], vq, sem, 0)
    for copy in copies:
        copy.start()
    rows, width = 8 * len(parts), gain.shape[1]
    scale = inverse_rms(lambda c: rows_at(parts, c), rows, width)
    for copy in copies:
        copy.wait()

    def step(c, totals):
        at = columns(c)
        normed = (rows_at(parts, c) * scale * gain[:, at].astype(f32)).astype(bf16)
        return (
            totals[0] + jnp.dot(normed, vq[at, :], preferred_element_type=f32),
            totals[1] + lax.dot_general(normed, wkv[:, at], NT, preferred_element_type=f32),
        )

    zeros = (jnp.zeros(q.shape, f32), jnp.zeros(pair.shape, f32))
    totals = lax.fori_loop(0, width // CHUNK, step, zeros)
    q[...] = totals[0].astype(bf16)
    pair[...] = totals[1].astype(bf16)


def project(place, parts, gain, wq, wkv):
    rows = 8 * len(parts)
    return pl.pallas_call(
        project_kernel,
        in_specs=[smem_spec()] + [vmem_spec()] * 5 + [any_spec(), vmem_spec()],
        out_specs=[vmem_spec()] * 2,
        out_shape=[
            jax.ShapeDtypeStruct((rows, wq.shape[1]), bf16),
            jax.ShapeDtypeStruct((rows, wkv.shape[0]), bf16),
        ],
        scratch_shapes=[pltpu.VMEM(wq.shape, bf16), pltpu.SemaphoreType.DMA((SPLIT,))],
        compiler_params=pltpu.CompilerParams(vmem_limit_bytes=16 * MIB),
        name="project",
    )(place, *parts, gain, wq, wkv)


def attention_kernel(blocks, copies_of, counts, ready, place, *refs):
    take = Taker(refs)
    if ready:
        (q_ref,) = take(1)
        pairs = take(4)
        (bounds,) = take(1)
    else:
        parts = take(blocks)
        gain, bounds = take(2)
        wq = [take(n) for n in counts]
    wo = [take(n) for n in counts]
    if not ready:
        wkv = take(4)
    (cache,) = take(1)
    outs = take(blocks)
    if not ready:
        vq, vkv = take(2)
    vo, vk, vv, sems = take(4)
    head, z = place[0], place[1]
    rows = 8 * blocks
    q_copies, kv_copies = [], []
    if not ready:
        q_copies = [piece_copies(wq[w], vq.at[w], sems, w) for w in range(copies_of)]
        kv_copies = [
            pltpu.make_async_copy(wkv[j].at[p], vkv.at[p, (z + 4 - j) % 4], sems.at[8 * SPLIT + 4 * p + j])
            for p in range(2)
            for j in range(4)
        ]
    if blocks == 4:
        k_copy = pltpu.make_async_copy(cache.at[:, :, 0, head], vk, sems.at[8 * SPLIT + 8])
        v_copy = pltpu.make_async_copy(cache.at[:, :, 1, head], vv, sems.at[8 * SPLIT + 9])
    else:
        own = pl.ds((z % 2) * 8, 8)
        k_copy = pltpu.make_async_copy(cache.at[z // 2, own, 0, head], vk.at[0], sems.at[8 * SPLIT + 8])
        v_copy = pltpu.make_async_copy(cache.at[z // 2, own, 1, head], vv.at[0], sems.at[8 * SPLIT + 9])
    o_copies = [piece_copies(wo[w], vo.at[w], sems, 4 + w) for w in range(copies_of)]
    for copy in sum(q_copies, []) + kv_copies + [k_copy, v_copy] + sum(o_copies, []):
        copy.start()
    queries = []
    if ready:
        q = q_ref[...].astype(f32)
        queries = [q[:, h * HD : (h + 1) * HD] for h in range(q.shape[1] // HD)]
        new = []
        for p in range(2):
            total = None
            for j in range(4):
                at_r = lax.broadcasted_iota(jnp.int32, (HD // 4, HD), 0)
                at_c = lax.broadcasted_iota(jnp.int32, (HD // 4, HD), 1)
                spot = jnp.where(at_c == (z + 4 - j) % 4 * (HD // 4) + at_r, 1.0, 0.0).astype(bf16)
                term = jnp.dot(pairs[j][p], spot, preferred_element_type=f32)
                term = jnp.concatenate([term[(m - j) % 4 * 8 : (m - j) % 4 * 8 + 8] for m in range(4)], axis=0)
                total = term if total is None else total + term
            new.append(total)
        key, value = new
    else:
        width = gain.shape[1]
        scale = inverse_rms(lambda c: rows_at(parts, c), rows, width)
        for copy in sum(q_copies, []) + kv_copies:
            copy.wait()

        def step(c, totals):
            cut = columns(c)
            normed = (rows_at(parts, c) * scale * gain[:, cut].astype(f32)).astype(bf16)
            terms = [jnp.dot(normed, vq[w, cut, :], preferred_element_type=f32) for w in range(copies_of)]
            both = vkv[:, :, :, cut].reshape(2 * HD, CHUNK)
            terms.append(lax.dot_general(normed, both, NT, preferred_element_type=f32))
            return tuple(total + term for total, term in zip(totals, terms))

        zeros = jnp.zeros((rows, 2 * HD), f32)
        totals = lax.fori_loop(0, width // CHUNK, step, (zeros,) * (copies_of + 1))
        for w in range(copies_of):
            q = totals[w].astype(bf16).astype(f32)
            queries += [q[:, h * HD : (h + 1) * HD] for h in range(q.shape[1] // HD)]
        pair = totals[-1].astype(bf16).astype(f32)
        key, value = pair[:, :HD], pair[:, HD:]
    heads = len(queries)
    queries = jnp.concatenate(queries, axis=0)
    new_key = jnp.concatenate([key] * heads, axis=0)
    new_value = jnp.concatenate([value] * heads, axis=0)
    factor = HD ** (-0.5)
    own_score = jnp.sum(queries * new_key, axis=-1, keepdims=True) * factor
    k_copy.wait()
    scores = lax.dot_general(
        queries.astype(bf16), vk[...].reshape(-1, HD), NT, preferred_element_type=f32
    )
    scores = scores * factor
    at = lax.broadcasted_iota(jnp.int32, scores.shape, 1)
    live = (at >= bounds[0, :, 0:1]) & (at < bounds[1, :, 0:1])
    scores = jnp.where(live, scores, -1e30)
    peak = jnp.maximum(jnp.max(scores, axis=-1, keepdims=True), own_score)
    weights = jnp.where(live, jnp.exp(scores - peak), 0.0)
    own = jnp.exp(own_score - peak)
    whole = jnp.sum(weights, axis=-1, keepdims=True) + own
    weights = (weights / whole).astype(bf16)
    own = (own / whole).astype(bf16).astype(f32)
    v_copy.wait()
    mixed = jnp.dot(weights, vv[...].reshape(-1, HD), preferred_element_type=f32)
    mixed = mixed + own * new_value
    per = heads // copies_of
    mixed = [
        jnp.concatenate(
            [mixed[(w * per + h) * rows : (w * per + h + 1) * rows] for h in range(per)], axis=1
        ).astype(bf16)
        for w in range(copies_of)
    ]
    for copy in sum(o_copies, []):
        copy.wait()

    def emit(c, nothing):
        cut = columns(c)
        total = jnp.dot(mixed[0], vo[0, :, cut], preferred_element_type=f32)
        for w in range(1, copies_of):
            total = total + jnp.dot(mixed[w], vo[w, :, cut], preferred_element_type=f32)
        for j in range(blocks):
            outs[j][:, cut] = total[8 * j : 8 * j + 8].astype(bf16)
        return nothing

    lax.fori_loop(0, outs[0].shape[1] // CHUNK, emit, 0)


def attention(place, parts, gain, bounds, wq, wo, wkv, cache, given=None):
    copies_of, ready = len(wo), given is not None
    blocks = 4 if ready else len(parts)
    width = wo[0][0].shape[1]
    ctx, hd = cache.shape[4:]
    kv_rows = (2, 16) if blocks == 4 else (1, 8)
    flat_o, counts = lay_out(wo)
    shape_o = (copies_of, sum(x.shape[0] for x in wo[0]), width)
    if ready:
        early = [*given, bounds]
        late = [*flat_o, cache]
        scratch = []
    else:
        flat_q, _ = lay_out(wq)
        early = [*parts, gain, bounds]
        late = [*flat_q, *flat_o, *wkv, cache]
        scratch = [
            pltpu.VMEM((copies_of, sum(x.shape[0] for x in wq[0]), wq[0][0].shape[1]), bf16),
            pltpu.VMEM((2, 4, HD // 4, width), bf16),
        ]
    return pl.pallas_call(
        lambda *refs: attention_kernel(blocks, copies_of, counts, ready, *refs),
        in_specs=[smem_spec()] + [vmem_spec()] * len(early) + [any_spec()] * len(late),
        out_specs=[vmem_spec()] * blocks,
        out_shape=[jax.ShapeDtypeStruct((8, width), bf16)] * blocks,
        scratch_shapes=scratch
        + [
            pltpu.VMEM(shape_o, bf16),
            pltpu.VMEM(kv_rows + (ctx, hd), bf16),
            pltpu.VMEM(kv_rows + (ctx, hd), bf16),
            pltpu.SemaphoreType.DMA((8 * SPLIT + 10,)),
        ],
        compiler_params=pltpu.CompilerParams(vmem_limit_bytes=36 * MIB),
        name="attention",
    )(place, *early, *late)


def middle_kernel(state, first, second, third, fourth, gain, residual, entry):
    total = state[...].astype(f32)
    for part in (first, second, third, fourth):
        total = total + part[...].astype(f32)
    residual[...] = total
    scale = lax.rsqrt(jnp.mean(total * total, axis=-1, keepdims=True) + NORM_EPSILON)
    entry[...] = (total * scale * gain[...].astype(f32)).astype(bf16)


def middle(state, parts, gain):
    return pl.pallas_call(
        middle_kernel,
        in_specs=[vmem_spec()] * 6,
        out_specs=[vmem_spec()] * 2,
        out_shape=[jax.ShapeDtypeStruct(state.shape, f32), jax.ShapeDtypeStruct(state.shape, bf16)],
        compiler_params=pltpu.CompilerParams(vmem_limit_bytes=8 * MIB),
        name="middle",
    )(state, *parts, gain)


def expert_kernel(blocks, copies_of, counts, place, *refs):
    take = Taker(refs)
    parts = take(blocks)
    router, chosen = take(2)
    weights = [take(n) for n in counts]
    outs = take(blocks)
    vw, sems = take(2)
    units = vw.shape[1] // 3
    copies = [piece_copies(weights[w], vw.at[w], sems, w) for w in range(copies_of)]
    for copy in sum(copies, []):
        copy.start()
    rows, width = 8 * blocks, router.shape[1]
    for copy in sum(copies, []):
        copy.wait()

    def step(c, totals):
        cut = columns(c)
        wide = rows_at(parts, c)
        entry = wide.astype(bf16)
        logits = [totals[i] + wide * router[i : i + 1, cut].astype(f32) for i in range(EXPS)]
        terms = [
            totals[EXPS + w]
            + lax.dot_general(entry, vw[w, 0 : 2 * units, cut], NT, preferred_element_type=f32)
            for w in range(copies_of)
        ]
        return tuple(logits + terms)

    zeros = (jnp.zeros((rows, CHUNK), f32),) * EXPS + (jnp.zeros((rows, 2 * units), f32),) * copies_of
    totals = lax.fori_loop(0, width // CHUNK, step, zeros)
    first = jnp.sum(totals[0], axis=-1, keepdims=True)
    second = jnp.sum(totals[1], axis=-1, keepdims=True)
    peak = jnp.maximum(first, second)
    first = jnp.exp(first - peak)
    second = jnp.exp(second - peak)
    expert = place[2]
    prob = jnp.where(expert == 0, first, second) / (first + second)
    mine = jnp.where(chosen[:, 0:1] == expert, prob, 0.0)
    hidden = []
    for w in range(copies_of):
        gate, upper = totals[EXPS + w][:, :units], totals[EXPS + w][:, units:]
        hidden.append((gate * jax.nn.sigmoid(gate) * upper).astype(bf16))

    def emit(c, nothing):
        cut = columns(c)
        total = jnp.dot(hidden[0], vw[0, 2 * units :, cut], preferred_element_type=f32)
        for w in range(1, copies_of):
            total = total + jnp.dot(hidden[w], vw[w, 2 * units :, cut], preferred_element_type=f32)
        total = total * mine
        for j in range(blocks):
            outs[j][:, cut] = total[8 * j : 8 * j + 8].astype(bf16)
        return nothing

    lax.fori_loop(0, width // CHUNK, emit, 0)


def experts(place, parts, router, chosen, weights):
    blocks, copies_of = len(parts), len(weights)
    flat, counts = lay_out(weights)
    width = flat[0].shape[1]
    total = sum(x.shape[0] for x in weights[0])
    return pl.pallas_call(
        lambda *refs: expert_kernel(blocks, copies_of, counts, *refs),
        in_specs=[smem_spec()] + [vmem_spec()] * (blocks + 2) + [any_spec()] * len(flat),
        out_specs=[vmem_spec()] * blocks,
        out_shape=[jax.ShapeDtypeStruct(parts[0].shape, bf16)] * blocks,
        scratch_shapes=[
            pltpu.VMEM((copies_of, total, width), bf16),
            pltpu.SemaphoreType.DMA((SPLIT * copies_of,)),
        ],
        compiler_params=pltpu.CompilerParams(vmem_limit_bytes=36 * MIB),
        name="experts",
    )(place, *parts, router, chosen, *flat)


def blank_kernel(*refs):
    pass


def blank(shapes):
    return pl.pallas_call(
        blank_kernel,
        out_specs=[any_spec()] * len(shapes),
        out_shape=[jax.ShapeDtypeStruct(shape, bf16) for shape in shapes],
        name="blank",
    )()


def sum_parts(parts):
    total = parts[0].astype(f32)
    for part in parts[1:]:
        total = total + part.astype(f32)
    return total


def gather_z(block):
    return [block] + [send(block, lambda s, x, z, k=k: (s, x, z + k)) for k in (1, 2, 3)]


def scatter_z(blocks):
    return sum_parts(
        [blocks[0]] + [send(blocks[j], lambda s, x, z, j=j: (s, x, z - j)) for j in (2, 1, 3)]
    ).astype(bf16)


def around_x(block):
    return [block] + [send(block, lambda s, x, z, k=k: (s, x + k, z)) for k in (2, 1, 3)]


def local(
    fresh_rows,
    row_bounds,
    layer_section,
    rows_in,
    attn_norm,
    q_proj,
    kv_proj,
    o_proj,
    kv_cache,
    cache_lengths,
    moe_norm,
    router,
    expert_ids,
):
    sections = lax.axis_size("section")
    shards = lax.axis_size("shard")
    section_pos = lax.axis_index("section")
    shard_pos = lax.axis_index("shard")
    x_pos = shard_pos // 4
    z_pos = shard_pos % 4
    width = rows_in.shape[2]

    pieces = fresh_rows[0, 0]
    layer_ids = jnp.arange(layer_section.shape[0], dtype=jnp.int32)
    order = jnp.sum(
        jnp.where(layer_section[None, :] == layer_ids[:, None], layer_ids[None, :], 0), axis=1
    ).astype(jnp.int32)
    owner = section_pos * shards + shard_pos
    base = (PIECE * owner).astype(jnp.int32)
    starts = lax.dynamic_slice_in_dim(row_bounds, owner, 1, 1)[:, 0]
    ends = lax.dynamic_slice_in_dim(row_bounds, owner + 1, 1, 1)[:, 0]
    slot = jnp.arange(pieces.shape[1], dtype=jnp.int32)[None, None, :]
    edge = jnp.arange(EDGE, dtype=jnp.int32)[None, :, None]
    pick = (slot == edge + (base + PIECE - starts)[:, None, None]).astype(bf16)
    count = sections * shards
    up = [(i, (i + 1) % count) for i in range(count)]
    down = [((i + 1) % count, i) for i in range(count)]

    to_right = jnp.einsum("lts,lsd->ltd", pick, pieces, preferred_element_type=f32).astype(bf16)
    from_left = lax.ppermute(to_right, AXES, up)
    from_right = lax.ppermute(pieces[:, :EDGE], AXES, down)

    micro, batch, _ = rows_in.shape
    rows = micro * batch
    heads_dev = q_proj.shape[2] // HD
    ctx = kv_cache.shape[5]
    shared_head = shard_pos * heads_dev // (HEADS // KVH)
    expert_pos = shard_pos // (shards // EXPS)
    place = jnp.stack([shared_head, z_pos, expert_pos, x_pos]).astype(jnp.int32)
    block_at = (z_pos - jnp.arange(4, dtype=jnp.int32)) % 4
    row_at = (block_at[:, None] * 8 + jnp.arange(8, dtype=jnp.int32)[None, :]).reshape(rows)
    lengths = jnp.take(cache_lengths.reshape(rows), row_at)
    low = row_at * ctx
    wide = (2, heads_dev, rows, HD)
    bounds = jnp.broadcast_to(jnp.stack((low, low + lengths))[:, None, :, None], wide).reshape(2, -1, HD)
    own_low = jnp.arange(8, dtype=jnp.int32) * ctx
    wide = (2, 4 * heads_dev, 8, HD)
    own_bounds = jnp.broadcast_to(
        jnp.stack((own_low, own_low + lengths[:8]))[:, None, :, None], wide
    ).reshape(2, -1, HD)
    router_rows = router[0].T
    chosen = jnp.broadcast_to(jnp.take(expert_ids[0].reshape(rows), row_at)[:, None], (rows, HD))
    entry_rows = rows_in.reshape(rows, width)
    entry_blocks = [lax.dynamic_slice_in_dim(entry_rows, 8 * block_at[j], 8, 0) for j in range(4)]
    own_kv = kv_proj[0].T
    shift = {0: 1, 1: 2, 2: 0, 3: 3}
    cross = {0: 0, 1: 3, 2: 1, 3: 2}

    def key_value(own):
        pair_a = send(own, lambda s, x, z: (s, shift[x], z))
        pair_b = send(own, lambda s, x, z: (s, cross[x], z))
        keys = jnp.where(x_pos == 0, own, jnp.where(x_pos == 3, pair_b, pair_a))
        values = jnp.where(x_pos == 0, pair_a, jnp.where(x_pos == 3, own, pair_b))
        return jnp.stack((keys, values), axis=0)

    def first_attention(state):
        q, pair = project(place, entry_blocks, attn_norm, q_proj[0], own_kv)
        pairs = gather_z(key_value(pair))
        blocks = attention(
            place, None, None, bounds, None, [[o_proj[0]]], None, kv_cache[0], given=[q, *pairs]
        )
        return middle(state, around_x(scatter_z(blocks)), moe_norm)

    (entry_blocks, own_kv, bounds, own_bounds, chosen, router_rows, place, from_left) = lax.optimization_barrier(
        (entry_blocks, own_kv, bounds, own_bounds, chosen, router_rows, place, from_left)
    )
    shares = build_shares(order, starts, ends, base[None], pieces, from_left, from_right)
    arrived = lax.all_to_all(shares, "section", split_axis=0, concat_axis=0, tiled=True)
    dest_rows = arrived.reshape(sections * PIECE, width)
    state, _ = lax.optimization_barrier((entry_blocks[0], shares))
    residual, entry = lax.cond(
        section_pos == 0, first_attention, lambda state: (state.astype(f32), state), state
    )

    q_own, o_own = q_proj[0], o_proj[0]

    def ring_copies(own):
        half = own.shape[0] // 2
        behind = send(own, lambda s, x, z: (s, x, z + 1))
        ahead = send(own, lambda s, x, z: (s, x, z - 1))
        far_a = send(behind[:half], lambda s, x, z: (s, x, z + 1))
        far_b = send(ahead[half:], lambda s, x, z: (s, x, z - 1))
        return behind, ahead, far_a, far_b

    def ring_shapes(own):
        half = (own.shape[0] // 2, own.shape[1])
        return [own.shape, own.shape, half, half]

    def with_own(own, copies):
        behind, ahead, far_a, far_b = copies
        return [[own], [behind], [ahead], [far_a, far_b]]

    copy_shapes = ring_shapes(q_own) + ring_shapes(o_own)

    def pair_only(own_kv):
        return (*gather_z(key_value(own_kv)), *blank(copy_shapes))

    def with_copies(own_kv):
        return (*gather_z(key_value(own_kv)), *ring_copies(q_own), *ring_copies(o_own))

    def no_copies(own_kv):
        return tuple(blank([(2,) + own_kv.shape] * 4 + copy_shapes))

    def among(places):
        return sum([(section_pos == place).astype(jnp.int32) for place in places])

    own_kv, _ = lax.optimization_barrier((own_kv, entry))
    copies = lax.switch(
        among(range(1, sections)) + among(RING_ATTENTION), [no_copies, pair_only, with_copies], own_kv
    )
    pair_weight = copies[:4]
    q_ring, o_ring = with_own(q_own, copies[4:8]), with_own(o_own, copies[8:])

    def first_experts(residual, entry):
        blocks = experts(place, gather_z(entry), router_rows, chosen, [[dest_rows]])
        return sum_parts([residual] + around_x(scatter_z(blocks))).astype(bf16)

    entry, _ = lax.optimization_barrier((entry, pair_weight))
    state = lax.cond(section_pos == 0, first_experts, lambda residual, entry: entry, residual, entry)
    keep = state
    coded = scale = rows_ring = None
    for tick in range(1, sections):
        if tick == 1:
            source, _ = lax.optimization_barrier((dest_rows, state))
            copies = lax.cond(
                among(RING_EXPERTS) == 1,
                lambda rows: ring_copies(rows),
                lambda rows: tuple(blank(ring_shapes(dest_rows))),
                source,
            )
            state, copies = lax.optimization_barrier((state, copies))
            rows_ring = with_own(dest_rows, copies)
        def hop(state, odd=(tick - 1) % 2):
            return send(
                state, lambda s, x, z: ((s ^ 1) if odd == 0 else (s - 1 if s % 2 == 0 else s + 1), x, z)
            )

        state = lax.cond(
            (section_pos == tick - 1) | (section_pos == tick), hop, lambda state: state, state
        )
        if tick == 4:
            source, _ = lax.optimization_barrier((dest_rows, state))
            coded, scale = quantize(source)
            state, coded = lax.optimization_barrier((state, coded))

        def layer(state, tick=tick):
            if tick in RING_ATTENTION:
                blocks = attention(
                    place, [state], attn_norm, own_bounds, q_ring, o_ring, pair_weight, kv_cache[0]
                )
                summed = blocks[0]
            else:
                blocks = attention(
                    place, gather_z(state), attn_norm, bounds, [[q_own]], [[o_own]], pair_weight, kv_cache[0]
                )
                summed = scatter_z(blocks)
            residual, entry = middle(state, around_x(summed), moe_norm)
            if tick in RING_EXPERTS:
                summed = experts(place, [entry], router_rows, chosen[:8], rows_ring)[0]
            else:
                summed = scatter_z(experts(place, gather_z(entry), router_rows, chosen, [[dest_rows]]))
            return sum_parts([residual] + around_x(summed)).astype(bf16)

        state = lax.cond(section_pos == tick, layer, lambda state: state, state)
        keep = jnp.where(section_pos == tick, state, keep)
    blocks = gather_z(keep)
    whole = jnp.concatenate(blocks, axis=0)
    wanted = jnp.arange(micro, dtype=jnp.int32) * batch + shard_pos
    found = jnp.argmax(row_at[None, :] == wanted[:, None], axis=1)
    outputs = jnp.take(whole, found, axis=0)
    return (coded[None, None], scale[None, None], outputs[None, :, None])


def solution(mesh):
    return jax.shard_map(
        local,
        mesh=mesh,
        in_specs=(
            P("section", "shard", None, None, None),
            P(),
            P(),
            P(),
            P("section", None),
            P("section", None, "shard"),
            P("section", None, "shard"),
            P("section", "shard", None),
            P("section", None, None, None, None, None, None),
            P(),
            P("section", None),
            P("section", None, None),
            P("section", None, None),
        ),
        out_specs=(
            P("section", "shard", None, None),
            P("section", "shard", None, None),
            P("section", None, "shard", None),
        ),
        check_vma=False,
    )
```

```python
import jax
import jax.numpy as jnp
from jax import lax
from jax.experimental import pallas as pl
from jax.experimental.pallas import tpu as pltpu
from jax.sharding import PartitionSpec as P

HD = 128
HEADS = 32
KVH = 2
EXPS = 2
QB = 128
EDGE = 8
PIECE = 48
CODE_LIMIT = 448.0
NORM_EPSILON = 1e-06
MIB = 1024 * 1024
RING_ATTENTION = (3, 4, 5, 6, 7)
RING_EXPERTS = (3, 5, 6, 7)

bf16 = jnp.bfloat16
f32 = jnp.float32
NT = (((1,), (1,)), ((), ()))


def pairs_of(move):
    result = []
    for s in range(8):
        for x in range(4):
            for z in range(4):
                s2, x2, z2 = move(s, x, z)
                result.append((s * 16 + x * 4 + z, s2 % 8 * 16 + x2 % 4 * 4 + z2 % 4))
    return result


AXES = ("section", "shard")


def send(value, move):
    return lax.ppermute(value, AXES, pairs_of(move))


def share_kernel(order, starts, ends, base, piece_ref, left_ref, right_ref, out_ref):
    layer = order[pl.program_id(0)]
    first = starts[layer] - base[0]
    stop = ends[layer] - base[0]
    t = lax.broadcasted_iota(jnp.int32, (PIECE, 64), 0)
    r = lax.broadcasted_iota(jnp.int32, (PIECE, 64), 1)
    own = jnp.where((r == t - first) & (t < stop), 1.0, 0.0).astype(bf16)
    t = lax.broadcasted_iota(jnp.int32, (PIECE, 16), 0)
    r = lax.broadcasted_iota(jnp.int32, (PIECE, 16), 1)
    near = (r < EDGE) & (r == t) & (t < first)
    far = (r >= EDGE) & (r - EDGE == t - stop) & (t >= stop)
    rim = jnp.where(near | far, 1.0, 0.0).astype(bf16)

    rims = jnp.concatenate((left_ref[0].astype(f32), right_ref[0].astype(f32)), axis=0).astype(bf16)
    total = jnp.dot(own, piece_ref[0], preferred_element_type=f32)
    total = total + jnp.dot(rim, rims, preferred_element_type=f32)
    out_ref[0] = total.astype(bf16)


def build_shares(order, starts, ends, base, pieces, from_left, from_right):
    layers, slots, width = pieces.shape
    return pl.pallas_call(
        share_kernel,
        grid_spec=pltpu.PrefetchScalarGridSpec(
            num_scalar_prefetch=4,
            grid=(layers,),
            in_specs=[
                pl.BlockSpec((1, slots, width), lambda d, o, *_: (o[d], 0, 0)),
                pl.BlockSpec((1, EDGE, width), lambda d, o, *_: (o[d], 0, 0)),
                pl.BlockSpec((1, EDGE, width), lambda d, o, *_: (o[d], 0, 0)),
            ],
            out_specs=pl.BlockSpec((1, PIECE, width), lambda d, *_: (d, 0, 0)),
        ),
        out_shape=jax.ShapeDtypeStruct((layers, PIECE, width), bf16),
        compiler_params=pltpu.CompilerParams(vmem_limit_bytes=24 * MIB),
        name="build_shares",
    )(order, starts, ends, base, pieces, from_left, from_right)


def quantize_kernel(rows_ref, coded_ref, scale_ref):
    step = pl.program_id(0)
    rows, width = rows_ref.shape
    cols = width // QB
    at_r = lax.broadcasted_iota(jnp.int32, scale_ref.shape, 0)
    at_c = lax.broadcasted_iota(jnp.int32, scale_ref.shape, 1)
    scales = jnp.where(step == 0, jnp.zeros(scale_ref.shape, f32), scale_ref[...])

    for c in range(cols):
        at = slice(c * QB, (c + 1) * QB)
        for i in range(rows // QB):
            tile = rows_ref[i * QB : (i + 1) * QB, at].astype(f32)
            peak = jnp.max(jnp.max(jnp.abs(tile), axis=0, keepdims=True), axis=1, keepdims=True)
            scale = (peak + 1e-06) / CODE_LIMIT
            coded_ref[i * QB : (i + 1) * QB, at] = (tile * (1.0 / scale)).astype(bf16)
            scales = jnp.where((at_r == i) & (at_c == step * cols + c), scale, scales)
    scale_ref[...] = scales


def quantize(rows):
    count, width = rows.shape
    chunk = 1024
    return pl.pallas_call(
        quantize_kernel,
        grid=(width // chunk,),
        in_specs=[pl.BlockSpec((count, chunk), lambda i: (0, i))],
        out_specs=[
            pl.BlockSpec((count, chunk), lambda i: (0, i)),
            pl.BlockSpec((count // QB, width // QB), lambda i: (0, 0)),
        ],
        out_shape=[
            jax.ShapeDtypeStruct((count, width), bf16),
            jax.ShapeDtypeStruct((count // QB, width // QB), f32),
        ],
        compiler_params=pltpu.CompilerParams(vmem_limit_bytes=24 * MIB),
        name="quantize",
    )(rows)


CHUNK = 2048


def rows_at(refs, c):
    at = pl.ds(pl.multiple_of(c * CHUNK, CHUNK), CHUNK)
    return jnp.concatenate([ref[:, at].astype(f32) for ref in refs], axis=0)


def columns(c):
    return pl.ds(pl.multiple_of(c * CHUNK, CHUNK), CHUNK)


def inverse_rms(load, rows, width):
    def add(c, total):
        wide = load(c)
        return total + wide * wide

    total = lax.fori_loop(0, width // CHUNK, add, jnp.zeros((rows, CHUNK), f32))
    return lax.rsqrt(jnp.sum(total, axis=-1, keepdims=True) / width + NORM_EPSILON)


def any_spec():
    return pl.BlockSpec(memory_space=pltpu.HBM)


def smem_spec():
    return pl.BlockSpec(memory_space=pltpu.SMEM)


def vmem_spec():
    return pl.BlockSpec(memory_space=pltpu.VMEM)


SPLIT = 4


def piece_copies(pieces, target, sems, first):
    copies, at = [], 0
    parts = SPLIT // len(pieces)
    for i, piece in enumerate(pieces):
        size = piece.shape[0] // parts
        for j in range(parts):
            copies.append(
                pltpu.make_async_copy(
                    piece.at[pl.ds(j * size, size)],
                    target.at[pl.ds(at, size)],
                    sems.at[first * SPLIT + i * parts + j],
                )
            )
            at += size
    return copies


class Taker:
    def __init__(self, refs):
        self.refs = list(refs)

    def __call__(self, count):
        result = self.refs[:count]
        del self.refs[:count]
        return result


def lay_out(lists):
    return [x for pieces in lists for x in pieces], [len(pieces) for pieces in lists]


def project_kernel(place, *refs):
    take = Taker(refs)
    parts = take(4)
    gain, wq, wkv, q, pair, vq, sem = take(7)
    del place
    copies = piece_copies([wq], vq, sem, 0)
    for copy in copies:
        copy.start()
    rows, width = 8 * len(parts), gain.shape[1]
    scale = inverse_rms(lambda c: rows_at(parts, c), rows, width)
    for copy in copies:
        copy.wait()

    def step(c, totals):
        at = columns(c)
        normed = (rows_at(parts, c) * scale * gain[:, at].astype(f32)).astype(bf16)
        return (
            totals[0] + jnp.dot(normed, vq[at, :], preferred_element_type=f32),
            totals[1] + lax.dot_general(normed, wkv[:, at], NT, preferred_element_type=f32),
        )

    zeros = (jnp.zeros(q.shape, f32), jnp.zeros(pair.shape, f32))
    totals = lax.fori_loop(0, width // CHUNK, step, zeros)
    q[...] = totals[0].astype(bf16)
    pair[...] = totals[1].astype(bf16)


def project(place, parts, gain, wq, wkv):
    rows = 8 * len(parts)
    return pl.pallas_call(
        project_kernel,
        in_specs=[smem_spec()] + [vmem_spec()] * 5 + [any_spec(), vmem_spec()],
        out_specs=[vmem_spec()] * 2,
        out_shape=[
            jax.ShapeDtypeStruct((rows, wq.shape[1]), bf16),
            jax.ShapeDtypeStruct((rows, wkv.shape[0]), bf16),
        ],
        scratch_shapes=[pltpu.VMEM(wq.shape, bf16), pltpu.SemaphoreType.DMA((SPLIT,))],
        compiler_params=pltpu.CompilerParams(vmem_limit_bytes=16 * MIB),
        name="project",
    )(place, *parts, gain, wq, wkv)


def attention_kernel(blocks, copies_of, counts, ready, place, *refs):
    take = Taker(refs)
    if ready:
        (q_ref,) = take(1)
        pairs = take(4)
        (bounds,) = take(1)
    else:
        parts = take(blocks)
        gain, bounds = take(2)
        wq = [take(n) for n in counts]
    wo = [take(n) for n in counts]
    if not ready:
        wkv = take(4)
    (cache,) = take(1)
    outs = take(blocks)
    if not ready:
        vq, vkv = take(2)
    vo, vk, vv, sems = take(4)
    head, z = place[0], place[1]
    rows = 8 * blocks
    q_copies, kv_copies = [], []
    if not ready:
        q_copies = [piece_copies(wq[w], vq.at[w], sems, w) for w in range(copies_of)]
        kv_copies = [
            pltpu.make_async_copy(wkv[j].at[p], vkv.at[p, (z + 4 - j) % 4], sems.at[8 * SPLIT + 4 * p + j])
            for p in range(2)
            for j in range(4)
        ]
    if blocks == 4:
        k_copy = pltpu.make_async_copy(cache.at[:, :, 0, head], vk, sems.at[8 * SPLIT + 8])
        v_copy = pltpu.make_async_copy(cache.at[:, :, 1, head], vv, sems.at[8 * SPLIT + 9])
    else:
        own = pl.ds((z % 2) * 8, 8)
        k_copy = pltpu.make_async_copy(cache.at[z // 2, own, 0, head], vk.at[0], sems.at[8 * SPLIT + 8])
        v_copy = pltpu.make_async_copy(cache.at[z // 2, own, 1, head], vv.at[0], sems.at[8 * SPLIT + 9])
    o_copies = [piece_copies(wo[w], vo.at[w], sems, 4 + w) for w in range(copies_of)]
    for copy in sum(q_copies, []) + kv_copies + [k_copy, v_copy] + sum(o_copies, []):
        copy.start()
    queries = []
    if ready:
        q = q_ref[...].astype(f32)
        queries = [q[:, h * HD : (h + 1) * HD] for h in range(q.shape[1] // HD)]
        new = []
        for p in range(2):
            total = None
            for j in range(4):
                at_r = lax.broadcasted_iota(jnp.int32, (HD // 4, HD), 0)
                at_c = lax.broadcasted_iota(jnp.int32, (HD // 4, HD), 1)
                spot = jnp.where(at_c == (z + 4 - j) % 4 * (HD // 4) + at_r, 1.0, 0.0).astype(bf16)
                term = jnp.dot(pairs[j][p], spot, preferred_element_type=f32)
                term = jnp.concatenate([term[(m - j) % 4 * 8 : (m - j) % 4 * 8 + 8] for m in range(4)], axis=0)
                total = term if total is None else total + term
            new.append(total)
        key, value = new
    else:
        width = gain.shape[1]
        scale = inverse_rms(lambda c: rows_at(parts, c), rows, width)
        for copy in sum(q_copies, []) + kv_copies:
            copy.wait()

        def step(c, totals):
            cut = columns(c)
            normed = (rows_at(parts, c) * scale * gain[:, cut].astype(f32)).astype(bf16)
            terms = [jnp.dot(normed, vq[w, cut, :], preferred_element_type=f32) for w in range(copies_of)]
            both = vkv[:, :, :, cut].reshape(2 * HD, CHUNK)
            terms.append(lax.dot_general(normed, both, NT, preferred_element_type=f32))
            return tuple(total + term for total, term in zip(totals, terms))

        zeros = jnp.zeros((rows, 2 * HD), f32)
        totals = lax.fori_loop(0, width // CHUNK, step, (zeros,) * (copies_of + 1))
        for w in range(copies_of):
            q = totals[w].astype(bf16).astype(f32)
            queries += [q[:, h * HD : (h + 1) * HD] for h in range(q.shape[1] // HD)]
        pair = totals[-1].astype(bf16).astype(f32)
        key, value = pair[:, :HD], pair[:, HD:]
    heads = len(queries)
    queries = jnp.concatenate(queries, axis=0)
    new_key = jnp.concatenate([key] * heads, axis=0)
    new_value = jnp.concatenate([value] * heads, axis=0)
    factor = HD ** (-0.5)
    own_score = jnp.sum(queries * new_key, axis=-1, keepdims=True) * factor
    k_copy.wait()
    scores = lax.dot_general(
        queries.astype(bf16), vk[...].reshape(-1, HD), NT, preferred_element_type=f32
    )
    scores = scores * factor
    at = lax.broadcasted_iota(jnp.int32, scores.shape, 1)
    live = (at >= bounds[0, :, 0:1]) & (at < bounds[1, :, 0:1])
    scores = jnp.where(live, scores, -1e30)
    peak = jnp.maximum(jnp.max(scores, axis=-1, keepdims=True), own_score)
    weights = jnp.where(live, jnp.exp(scores - peak), 0.0)
    own = jnp.exp(own_score - peak)
    whole = jnp.sum(weights, axis=-1, keepdims=True) + own
    weights = (weights / whole).astype(bf16)
    own = (own / whole).astype(bf16).astype(f32)
    v_copy.wait()
    mixed = jnp.dot(weights, vv[...].reshape(-1, HD), preferred_element_type=f32)
    mixed = mixed + own * new_value
    per = heads // copies_of
    mixed = [
        jnp.concatenate(
            [mixed[(w * per + h) * rows : (w * per + h + 1) * rows] for h in range(per)], axis=1
        ).astype(bf16)
        for w in range(copies_of)
    ]
    for copy in sum(o_copies, []):
        copy.wait()

    def emit(c, nothing):
        cut = columns(c)
        total = jnp.dot(mixed[0], vo[0, :, cut], preferred_element_type=f32)
        for w in range(1, copies_of):
            total = total + jnp.dot(mixed[w], vo[w, :, cut], preferred_element_type=f32)
        for j in range(blocks):
            outs[j][:, cut] = total[8 * j : 8 * j + 8].astype(bf16)
        return nothing

    lax.fori_loop(0, outs[0].shape[1] // CHUNK, emit, 0)


def attention(place, parts, gain, bounds, wq, wo, wkv, cache, given=None):
    copies_of, ready = len(wo), given is not None
    blocks = 4 if ready else len(parts)
    width = wo[0][0].shape[1]
    ctx, hd = cache.shape[4:]
    kv_rows = (2, 16) if blocks == 4 else (1, 8)
    flat_o, counts = lay_out(wo)
    shape_o = (copies_of, sum(x.shape[0] for x in wo[0]), width)
    if ready:
        early = [*given, bounds]
        late = [*flat_o, cache]
        scratch = []
    else:
        flat_q, _ = lay_out(wq)
        early = [*parts, gain, bounds]
        late = [*flat_q, *flat_o, *wkv, cache]
        scratch = [
            pltpu.VMEM((copies_of, sum(x.shape[0] for x in wq[0]), wq[0][0].shape[1]), bf16),
            pltpu.VMEM((2, 4, HD // 4, width), bf16),
        ]
    return pl.pallas_call(
        lambda *refs: attention_kernel(blocks, copies_of, counts, ready, *refs),
        in_specs=[smem_spec()] + [vmem_spec()] * len(early) + [any_spec()] * len(late),
        out_specs=[vmem_spec()] * blocks,
        out_shape=[jax.ShapeDtypeStruct((8, width), bf16)] * blocks,
        scratch_shapes=scratch
        + [
            pltpu.VMEM(shape_o, bf16),
            pltpu.VMEM(kv_rows + (ctx, hd), bf16),
            pltpu.VMEM(kv_rows + (ctx, hd), bf16),
            pltpu.SemaphoreType.DMA((8 * SPLIT + 10,)),
        ],
        compiler_params=pltpu.CompilerParams(vmem_limit_bytes=36 * MIB),
        name="attention",
    )(place, *early, *late)


def middle_kernel(state, first, second, third, fourth, gain, residual, entry):
    total = state[...].astype(f32)
    for part in (first, second, third, fourth):
        total = total + part[...].astype(f32)
    residual[...] = total
    scale = lax.rsqrt(jnp.mean(total * total, axis=-1, keepdims=True) + NORM_EPSILON)
    entry[...] = (total * scale * gain[...].astype(f32)).astype(bf16)


def middle(state, parts, gain):
    return pl.pallas_call(
        middle_kernel,
        in_specs=[vmem_spec()] * 6,
        out_specs=[vmem_spec()] * 2,
        out_shape=[jax.ShapeDtypeStruct(state.shape, f32), jax.ShapeDtypeStruct(state.shape, bf16)],
        compiler_params=pltpu.CompilerParams(vmem_limit_bytes=8 * MIB),
        name="middle",
    )(state, *parts, gain)


def expert_kernel(blocks, copies_of, counts, fused, place, *refs):
    take = Taker(refs)
    if fused:
        inputs = take(6)
    else:
        parts = take(blocks)
    router, chosen = take(2)
    weights = [take(n) for n in counts]
    outs = take(blocks)
    if fused:
        (residual,) = take(1)
    vw, sems = take(2)
    if fused:
        parts = take(1)
    units = vw.shape[1] // 3
    copies = [piece_copies(weights[w], vw.at[w], sems, w) for w in range(copies_of)]
    for copy in sum(copies, []):
        copy.start()
    rows, width = 8 * blocks, router.shape[1]
    if fused:
        middle_kernel(*inputs, residual, parts[0])
    for copy in sum(copies, []):
        copy.wait()

    def step(c, totals):
        cut = columns(c)
        wide = rows_at(parts, c)
        entry = wide.astype(bf16)
        logits = [totals[i] + wide * router[i : i + 1, cut].astype(f32) for i in range(EXPS)]
        terms = [
            totals[EXPS + w]
            + lax.dot_general(entry, vw[w, 0 : 2 * units, cut], NT, preferred_element_type=f32)
            for w in range(copies_of)
        ]
        return tuple(logits + terms)

    zeros = (jnp.zeros((rows, CHUNK), f32),) * EXPS + (jnp.zeros((rows, 2 * units), f32),) * copies_of
    totals = lax.fori_loop(0, width // CHUNK, step, zeros)
    first = jnp.sum(totals[0], axis=-1, keepdims=True)
    second = jnp.sum(totals[1], axis=-1, keepdims=True)
    peak = jnp.maximum(first, second)
    first = jnp.exp(first - peak)
    second = jnp.exp(second - peak)
    expert = place[2]
    prob = jnp.where(expert == 0, first, second) / (first + second)
    mine = jnp.where(chosen[:, 0:1] == expert, prob, 0.0)
    hidden = []
    for w in range(copies_of):
        gate, upper = totals[EXPS + w][:, :units], totals[EXPS + w][:, units:]
        hidden.append((gate * jax.nn.sigmoid(gate) * upper).astype(bf16))

    def emit(c, nothing):
        cut = columns(c)
        total = jnp.dot(hidden[0], vw[0, 2 * units :, cut], preferred_element_type=f32)
        for w in range(1, copies_of):
            total = total + jnp.dot(hidden[w], vw[w, 2 * units :, cut], preferred_element_type=f32)
        total = total * mine
        for j in range(blocks):
            outs[j][:, cut] = total[8 * j : 8 * j + 8].astype(bf16)
        return nothing

    lax.fori_loop(0, width // CHUNK, emit, 0)


def experts(place, parts, router, chosen, weights, fused=None):
    blocks, copies_of = 1 if fused else len(parts), len(weights)
    flat, counts = lay_out(weights)
    width = flat[0].shape[1]
    total = sum(x.shape[0] for x in weights[0])
    early = fused or parts
    outs = [jax.ShapeDtypeStruct((8, width), bf16)] * blocks
    scratch = [
        pltpu.VMEM((copies_of, total, width), bf16),
        pltpu.SemaphoreType.DMA((SPLIT * copies_of,)),
    ]
    if fused:
        outs.append(jax.ShapeDtypeStruct((8, width), f32))
        scratch.append(pltpu.VMEM((8, width), bf16))
    return pl.pallas_call(
        lambda *refs: expert_kernel(blocks, copies_of, counts, bool(fused), *refs),
        in_specs=[smem_spec()] + [vmem_spec()] * (len(early) + 2) + [any_spec()] * len(flat),
        out_specs=[vmem_spec()] * len(outs),
        out_shape=outs,
        scratch_shapes=scratch,
        compiler_params=pltpu.CompilerParams(vmem_limit_bytes=36 * MIB),
        name="experts",
    )(place, *early, router, chosen, *flat)


def blank_kernel(*refs):
    pass


def blank(shapes):
    return pl.pallas_call(
        blank_kernel,
        out_specs=[any_spec()] * len(shapes),
        out_shape=[jax.ShapeDtypeStruct(shape, bf16) for shape in shapes],
        name="blank",
    )()


def sum_parts(parts):
    total = parts[0].astype(f32)
    for part in parts[1:]:
        total = total + part.astype(f32)
    return total


def gather_z(block):
    return [block] + [send(block, lambda s, x, z, k=k: (s, x, z + k)) for k in (1, 2, 3)]


def scatter_z(blocks):
    return sum_parts(
        [blocks[0]] + [send(blocks[j], lambda s, x, z, j=j: (s, x, z - j)) for j in (2, 1, 3)]
    ).astype(bf16)


def around_x(block):
    return [block] + [send(block, lambda s, x, z, k=k: (s, x + k, z)) for k in (2, 1, 3)]


def local(
    fresh_rows,
    row_bounds,
    layer_section,
    rows_in,
    attn_norm,
    q_proj,
    kv_proj,
    o_proj,
    kv_cache,
    cache_lengths,
    moe_norm,
    router,
    expert_ids,
):
    sections = lax.axis_size("section")
    shards = lax.axis_size("shard")
    section_pos = lax.axis_index("section")
    shard_pos = lax.axis_index("shard")
    x_pos = shard_pos // 4
    z_pos = shard_pos % 4
    width = rows_in.shape[2]

    pieces = fresh_rows[0, 0]
    layer_ids = jnp.arange(layer_section.shape[0], dtype=jnp.int32)
    order = jnp.sum(
        jnp.where(layer_section[None, :] == layer_ids[:, None], layer_ids[None, :], 0), axis=1
    ).astype(jnp.int32)
    owner = section_pos * shards + shard_pos
    base = (PIECE * owner).astype(jnp.int32)
    starts = lax.dynamic_slice_in_dim(row_bounds, owner, 1, 1)[:, 0]
    ends = lax.dynamic_slice_in_dim(row_bounds, owner + 1, 1, 1)[:, 0]
    slot = jnp.arange(pieces.shape[1], dtype=jnp.int32)[None, None, :]
    edge = jnp.arange(EDGE, dtype=jnp.int32)[None, :, None]
    pick = (slot == edge + (base + PIECE - starts)[:, None, None]).astype(bf16)
    count = sections * shards
    up = [(i, (i + 1) % count) for i in range(count)]
    down = [((i + 1) % count, i) for i in range(count)]

    to_right = jnp.einsum("lts,lsd->ltd", pick, pieces, preferred_element_type=f32).astype(bf16)
    from_left = lax.ppermute(to_right, AXES, up)
    from_right = lax.ppermute(pieces[:, :EDGE], AXES, down)

    micro, batch, _ = rows_in.shape
    rows = micro * batch
    heads_dev = q_proj.shape[2] // HD
    ctx = kv_cache.shape[5]
    shared_head = shard_pos * heads_dev // (HEADS // KVH)
    expert_pos = shard_pos // (shards // EXPS)
    place = jnp.stack([shared_head, z_pos, expert_pos, x_pos]).astype(jnp.int32)
    block_at = (z_pos - jnp.arange(4, dtype=jnp.int32)) % 4
    row_at = (block_at[:, None] * 8 + jnp.arange(8, dtype=jnp.int32)[None, :]).reshape(rows)
    lengths = jnp.take(cache_lengths.reshape(rows), row_at)
    low = row_at * ctx
    wide = (2, heads_dev, rows, HD)
    bounds = jnp.broadcast_to(jnp.stack((low, low + lengths))[:, None, :, None], wide).reshape(2, -1, HD)
    own_low = jnp.arange(8, dtype=jnp.int32) * ctx
    wide = (2, 4 * heads_dev, 8, HD)
    own_bounds = jnp.broadcast_to(
        jnp.stack((own_low, own_low + lengths[:8]))[:, None, :, None], wide
    ).reshape(2, -1, HD)
    router_rows = router[0].T
    chosen = jnp.broadcast_to(jnp.take(expert_ids[0].reshape(rows), row_at)[:, None], (rows, HD))
    entry_rows = rows_in.reshape(rows, width)
    entry_blocks = [lax.dynamic_slice_in_dim(entry_rows, 8 * block_at[j], 8, 0) for j in range(4)]
    own_kv = kv_proj[0].T
    shift = {0: 1, 1: 2, 2: 0, 3: 3}
    cross = {0: 0, 1: 3, 2: 1, 3: 2}

    def key_value(own):
        pair_a = send(own, lambda s, x, z: (s, shift[x], z))
        pair_b = send(own, lambda s, x, z: (s, cross[x], z))
        keys = jnp.where(x_pos == 0, own, jnp.where(x_pos == 3, pair_b, pair_a))
        values = jnp.where(x_pos == 0, pair_a, jnp.where(x_pos == 3, own, pair_b))
        return jnp.stack((keys, values), axis=0)

    def first_attention(state):
        q, pair = project(place, entry_blocks, attn_norm, q_proj[0], own_kv)
        pairs = gather_z(key_value(pair))
        blocks = attention(
            place, None, None, bounds, None, [[o_proj[0]]], None, kv_cache[0], given=[q, *pairs]
        )
        return middle(state, around_x(scatter_z(blocks)), moe_norm)

    (entry_blocks, own_kv, bounds, own_bounds, chosen, router_rows, place, from_left) = lax.optimization_barrier(
        (entry_blocks, own_kv, bounds, own_bounds, chosen, router_rows, place, from_left)
    )
    shares = build_shares(order, starts, ends, base[None], pieces, from_left, from_right)
    arrived = lax.all_to_all(shares, "section", split_axis=0, concat_axis=0, tiled=True)
    dest_rows = arrived.reshape(sections * PIECE, width)
    state, _ = lax.optimization_barrier((entry_blocks[0], shares))
    residual, entry = lax.cond(
        section_pos == 0, first_attention, lambda state: (state.astype(f32), state), state
    )

    q_own, o_own = q_proj[0], o_proj[0]

    def ring_copies(own):
        half = own.shape[0] // 2
        behind = send(own, lambda s, x, z: (s, x, z + 1))
        ahead = send(own, lambda s, x, z: (s, x, z - 1))
        far_a = send(behind[:half], lambda s, x, z: (s, x, z + 1))
        far_b = send(ahead[half:], lambda s, x, z: (s, x, z - 1))
        return behind, ahead, far_a, far_b

    def ring_shapes(own):
        half = (own.shape[0] // 2, own.shape[1])
        return [own.shape, own.shape, half, half]

    def with_own(own, copies):
        behind, ahead, far_a, far_b = copies
        return [[own], [behind], [ahead], [far_a, far_b]]

    copy_shapes = ring_shapes(q_own) + ring_shapes(o_own)

    def pair_only(own_kv):
        return (*gather_z(key_value(own_kv)), *blank(copy_shapes))

    def with_copies(own_kv):
        return (*gather_z(key_value(own_kv)), *ring_copies(q_own), *ring_copies(o_own))

    def no_copies(own_kv):
        return tuple(blank([(2,) + own_kv.shape] * 4 + copy_shapes))

    def among(places):
        return sum([(section_pos == place).astype(jnp.int32) for place in places])

    own_kv, _ = lax.optimization_barrier((own_kv, entry))
    copies = lax.switch(
        among(range(1, sections)) + among(RING_ATTENTION), [no_copies, pair_only, with_copies], own_kv
    )
    pair_weight = copies[:4]
    q_ring, o_ring = with_own(q_own, copies[4:8]), with_own(o_own, copies[8:])

    def first_experts(residual, entry, rows):
        blocks = experts(place, gather_z(entry), router_rows, chosen, [[rows]])
        state = sum_parts([residual] + around_x(scatter_z(blocks))).astype(bf16)
        return (state, *quantize(rows))

    def no_experts(residual, entry, rows):
        return (*blank([(8, width)]), *quantize(rows))

    entry, _ = lax.optimization_barrier((entry, pair_weight))
    state, coded, scale = lax.cond(section_pos == 0, first_experts, no_experts, residual, entry, dest_rows)
    keep = state
    source, _ = lax.optimization_barrier((dest_rows, state))
    copies = lax.cond(
        among(RING_EXPERTS) == 1,
        lambda rows: ring_copies(rows),
        lambda rows: tuple(blank(ring_shapes(dest_rows))),
        source,
    )
    state, copies = lax.optimization_barrier((state, copies))
    rows_ring = with_own(dest_rows, copies)

    def hop(tick):
        count = 1 if tick in RING_ATTENTION else 4

        def move(s, x, z, k):
            return ((s ^ 1) if tick % 2 else (s - 1 if s % 2 == 0 else s + 1), x, z + k)

        def run(state):
            return tuple(send(state, lambda s, x, z, k=k: move(s, x, z, k)) for k in range(count))

        return run

    def layer(tick):
        def run(*blocks):
            state = blocks[0]
            if tick in RING_ATTENTION:
                summed = attention(
                    place, [state], attn_norm, own_bounds, q_ring, o_ring, pair_weight, kv_cache[0]
                )[0]
            else:
                summed = scatter_z(
                    attention(
                        place, blocks, attn_norm, bounds, [[q_own]], [[o_own]], pair_weight, kv_cache[0]
                    )
                )
            if tick in RING_EXPERTS:
                summed, residual = experts(
                    place, None, router_rows, chosen[:8], rows_ring, fused=[state, *around_x(summed), moe_norm]
                )
            else:
                residual, entry = middle(state, around_x(summed), moe_norm)
                summed = scatter_z(experts(place, gather_z(entry), router_rows, chosen, [[dest_rows]]))
            return sum_parts([residual] + around_x(summed)).astype(bf16)

        return run

    def nothing(count):
        def run(*_):
            return tuple(blank([(8, width)] * count))

        return run

    def hop_to(tick, state):
        step = hop(tick)
        count = 1 if tick in RING_ATTENTION else 4
        return lax.cond(
            (section_pos == tick - 1) | (section_pos == tick), step, nothing(count), state
        )

    def at_layer(tick, blocks):
        step = layer(tick)
        return lax.cond(section_pos == tick, lambda *blocks: (step(*blocks),), nothing(1), *blocks)[0]

    state = at_layer(1, hop_to(1, state))
    keep = jnp.where(section_pos == 1, state, keep)
    for even in range(2, sections, 2):
        blocks = hop_to(even, state)
        here = (section_pos == even) | (section_pos == even + 1)

        def pair(*blocks, even=even):
            first = at_layer(even, blocks)
            second = at_layer(even + 1, hop(even + 1)(first))
            return (jnp.where(section_pos == even, first, second),)

        (state,) = lax.cond(here, pair, nothing(1), *blocks)
        keep = jnp.where(here, state, keep)
    blocks = gather_z(keep)
    whole = jnp.concatenate(blocks, axis=0)
    wanted = jnp.arange(micro, dtype=jnp.int32) * batch + shard_pos
    found = jnp.argmax(row_at[None, :] == wanted[:, None], axis=1)
    outputs = jnp.take(whole, found, axis=0)
    return (coded[None, None], scale[None, None], outputs[None, :, None])


def solution(mesh):
    return jax.shard_map(
        local,
        mesh=mesh,
        in_specs=(
            P("section", "shard", None, None, None),
            P(),
            P(),
            P(),
            P("section", None),
            P("section", None, "shard"),
            P("section", None, "shard"),
            P("section", "shard", None),
            P("section", None, None, None, None, None, None),
            P(),
            P("section", None),
            P("section", None, None),
            P("section", None, None),
        ),
        out_specs=(
            P("section", "shard", None, None),
            P("section", "shard", None, None),
            P("section", None, "shard", None),
        ),
        check_vma=False,
    )
```

```python
import jax
import jax.numpy as jnp
from jax import lax
from jax.experimental import pallas as pl
from jax.experimental.pallas import tpu as pltpu
from jax.sharding import PartitionSpec as P

HD = 128
HEADS = 32
KVH = 2
EXPS = 2
QB = 128
EDGE = 8
PIECE = 48
CODE_LIMIT = 448.0
NORM_EPSILON = 1e-06
MIB = 1024 * 1024
RING_ATTENTION = (3, 4, 5, 6, 7)
RING_EXPERTS = (3, 5, 6, 7)

bf16 = jnp.bfloat16
f32 = jnp.float32
NT = (((1,), (1,)), ((), ()))


def pairs_of(move):
    result = []
    for s in range(8):
        for x in range(4):
            for z in range(4):
                s2, x2, z2 = move(s, x, z)
                result.append((s * 16 + x * 4 + z, s2 % 8 * 16 + x2 % 4 * 4 + z2 % 4))
    return result


AXES = ("section", "shard")


def send(value, move):
    return lax.ppermute(value, AXES, pairs_of(move))


def share_kernel(order, starts, ends, base, piece_ref, left_ref, right_ref, out_ref):
    layer = order[pl.program_id(0)]
    first = starts[layer] - base[0]
    stop = ends[layer] - base[0]
    t = lax.broadcasted_iota(jnp.int32, (PIECE, 64), 0)
    r = lax.broadcasted_iota(jnp.int32, (PIECE, 64), 1)
    own = jnp.where((r == t - first) & (t < stop), 1.0, 0.0).astype(bf16)
    t = lax.broadcasted_iota(jnp.int32, (PIECE, 16), 0)
    r = lax.broadcasted_iota(jnp.int32, (PIECE, 16), 1)
    near = (r < EDGE) & (r == t) & (t < first)
    far = (r >= EDGE) & (r - EDGE == t - stop) & (t >= stop)
    rim = jnp.where(near | far, 1.0, 0.0).astype(bf16)

    rims = jnp.concatenate((left_ref[0].astype(f32), right_ref[0].astype(f32)), axis=0).astype(bf16)
    total = jnp.dot(own, piece_ref[0], preferred_element_type=f32)
    total = total + jnp.dot(rim, rims, preferred_element_type=f32)
    out_ref[0] = total.astype(bf16)


def build_shares(order, starts, ends, base, pieces, from_left, from_right):
    layers, slots, width = pieces.shape
    return pl.pallas_call(
        share_kernel,
        grid_spec=pltpu.PrefetchScalarGridSpec(
            num_scalar_prefetch=4,
            grid=(layers,),
            in_specs=[
                pl.BlockSpec((1, slots, width), lambda d, o, *_: (o[d], 0, 0)),
                pl.BlockSpec((1, EDGE, width), lambda d, o, *_: (o[d], 0, 0)),
                pl.BlockSpec((1, EDGE, width), lambda d, o, *_: (o[d], 0, 0)),
            ],
            out_specs=pl.BlockSpec((1, PIECE, width), lambda d, *_: (d, 0, 0)),
        ),
        out_shape=jax.ShapeDtypeStruct((layers, PIECE, width), bf16),
        compiler_params=pltpu.CompilerParams(vmem_limit_bytes=24 * MIB),
        name="build_shares",
    )(order, starts, ends, base, pieces, from_left, from_right)


def quantize_kernel(rows_ref, coded_ref, scale_ref):
    step = pl.program_id(0)
    rows, width = rows_ref.shape
    cols = width // QB
    at_r = lax.broadcasted_iota(jnp.int32, scale_ref.shape, 0)
    at_c = lax.broadcasted_iota(jnp.int32, scale_ref.shape, 1)
    scales = jnp.where(step == 0, jnp.zeros(scale_ref.shape, f32), scale_ref[...])

    for c in range(cols):
        at = slice(c * QB, (c + 1) * QB)
        for i in range(rows // QB):
            tile = rows_ref[i * QB : (i + 1) * QB, at].astype(f32)
            peak = jnp.max(jnp.max(jnp.abs(tile), axis=0, keepdims=True), axis=1, keepdims=True)
            scale = (peak + 1e-06) / CODE_LIMIT
            coded_ref[i * QB : (i + 1) * QB, at] = (tile * (1.0 / scale)).astype(bf16)
            scales = jnp.where((at_r == i) & (at_c == step * cols + c), scale, scales)
    scale_ref[...] = scales


def quantize(rows):
    count, width = rows.shape
    chunk = 1024
    return pl.pallas_call(
        quantize_kernel,
        grid=(width // chunk,),
        in_specs=[pl.BlockSpec((count, chunk), lambda i: (0, i))],
        out_specs=[
            pl.BlockSpec((count, chunk), lambda i: (0, i)),
            pl.BlockSpec((count // QB, width // QB), lambda i: (0, 0)),
        ],
        out_shape=[
            jax.ShapeDtypeStruct((count, width), bf16),
            jax.ShapeDtypeStruct((count // QB, width // QB), f32),
        ],
        compiler_params=pltpu.CompilerParams(vmem_limit_bytes=24 * MIB),
        name="quantize",
    )(rows)


CHUNK = 2048


def rows_at(refs, c):
    at = pl.ds(pl.multiple_of(c * CHUNK, CHUNK), CHUNK)
    return jnp.concatenate([ref[:, at].astype(f32) for ref in refs], axis=0)


def columns(c):
    return pl.ds(pl.multiple_of(c * CHUNK, CHUNK), CHUNK)


def inverse_rms(load, rows, width):
    def add(c, total):
        wide = load(c)
        return total + wide * wide

    total = lax.fori_loop(0, width // CHUNK, add, jnp.zeros((rows, CHUNK), f32))
    return lax.rsqrt(jnp.sum(total, axis=-1, keepdims=True) / width + NORM_EPSILON)


def any_spec():
    return pl.BlockSpec(memory_space=pltpu.HBM)


def smem_spec():
    return pl.BlockSpec(memory_space=pltpu.SMEM)


def vmem_spec():
    return pl.BlockSpec(memory_space=pltpu.VMEM)


SPLIT = 4
ROW_SPLIT = 6


def piece_copies(pieces, target, sems, first, split=SPLIT):
    copies, at = [], 0
    parts = split // len(pieces)
    for i, piece in enumerate(pieces):
        size = piece.shape[0] // parts
        for j in range(parts):
            copies.append(
                pltpu.make_async_copy(
                    piece.at[pl.ds(j * size, size)],
                    target.at[pl.ds(at, size)],
                    sems.at[first * split + i * parts + j],
                )
            )
            at += size
    return copies


class Taker:
    def __init__(self, refs):
        self.refs = list(refs)

    def __call__(self, count):
        result = self.refs[:count]
        del self.refs[:count]
        return result


def lay_out(lists):
    return [x for pieces in lists for x in pieces], [len(pieces) for pieces in lists]


def project_kernel(place, *refs):
    take = Taker(refs)
    parts = take(4)
    gain, wq, wkv, q, pair, vq, sem = take(7)
    del place
    copies = piece_copies([wq], vq, sem, 0)
    for copy in copies:
        copy.start()
    rows, width = 8 * len(parts), gain.shape[1]
    scale = inverse_rms(lambda c: rows_at(parts, c), rows, width)
    for copy in copies:
        copy.wait()

    def step(c, totals):
        at = columns(c)
        normed = (rows_at(parts, c) * scale * gain[:, at].astype(f32)).astype(bf16)
        return (
            totals[0] + jnp.dot(normed, vq[at, :], preferred_element_type=f32),
            totals[1] + lax.dot_general(normed, wkv[:, at], NT, preferred_element_type=f32),
        )

    zeros = (jnp.zeros(q.shape, f32), jnp.zeros(pair.shape, f32))
    totals = lax.fori_loop(0, width // CHUNK, step, zeros)
    q[...] = totals[0].astype(bf16)
    pair[...] = totals[1].astype(bf16)


def project(place, parts, gain, wq, wkv):
    rows = 8 * len(parts)
    return pl.pallas_call(
        project_kernel,
        in_specs=[smem_spec()] + [vmem_spec()] * 5 + [any_spec(), vmem_spec()],
        out_specs=[vmem_spec()] * 2,
        out_shape=[
            jax.ShapeDtypeStruct((rows, wq.shape[1]), bf16),
            jax.ShapeDtypeStruct((rows, wkv.shape[0]), bf16),
        ],
        scratch_shapes=[pltpu.VMEM(wq.shape, bf16), pltpu.SemaphoreType.DMA((SPLIT,))],
        compiler_params=pltpu.CompilerParams(vmem_limit_bytes=16 * MIB),
        name="project",
    )(place, *parts, gain, wq, wkv)


def attention_kernel(blocks, copies_of, counts, ready, place, *refs):
    take = Taker(refs)
    if ready:
        (q_ref,) = take(1)
        pairs = take(4)
        (bounds,) = take(1)
    else:
        parts = take(blocks)
        gain, bounds = take(2)
        wq = [take(n) for n in counts]
    wo = [take(n) for n in counts]
    if not ready:
        wkv = take(4)
    (cache,) = take(1)
    outs = take(blocks)
    if not ready:
        vq, vkv = take(2)
    vo, vk, vv, sems = take(4)
    head, z = place[0], place[1]
    rows = 8 * blocks
    q_copies, kv_copies = [], []
    if not ready:
        q_copies = [piece_copies(wq[w], vq.at[w], sems, w) for w in range(copies_of)]
        kv_copies = [
            pltpu.make_async_copy(wkv[j].at[p], vkv.at[p, (z + 4 - j) % 4], sems.at[8 * SPLIT + 4 * p + j])
            for p in range(2)
            for j in range(4)
        ]
    if blocks == 4:
        k_copy = pltpu.make_async_copy(cache.at[:, :, 0, head], vk, sems.at[8 * SPLIT + 8])
        v_copy = pltpu.make_async_copy(cache.at[:, :, 1, head], vv, sems.at[8 * SPLIT + 9])
    else:
        own = pl.ds((z % 2) * 8, 8)
        k_copy = pltpu.make_async_copy(cache.at[z // 2, own, 0, head], vk.at[0], sems.at[8 * SPLIT + 8])
        v_copy = pltpu.make_async_copy(cache.at[z // 2, own, 1, head], vv.at[0], sems.at[8 * SPLIT + 9])
    o_copies = [piece_copies(wo[w], vo.at[w], sems, 4 + w) for w in range(copies_of)]
    half = SPLIT // 2
    early = sum([copies[:half] for copies in q_copies], []) + kv_copies
    late = sum([copies[half:] for copies in q_copies], [])
    for copy in early + late + [k_copy, v_copy] + sum(o_copies, []):
        copy.start()
    queries = []
    if ready:
        q = q_ref[...].astype(f32)
        queries = [q[:, h * HD : (h + 1) * HD] for h in range(q.shape[1] // HD)]
        new = []
        for p in range(2):
            total = None
            for j in range(4):
                at_r = lax.broadcasted_iota(jnp.int32, (HD // 4, HD), 0)
                at_c = lax.broadcasted_iota(jnp.int32, (HD // 4, HD), 1)
                spot = jnp.where(at_c == (z + 4 - j) % 4 * (HD // 4) + at_r, 1.0, 0.0).astype(bf16)
                term = jnp.dot(pairs[j][p], spot, preferred_element_type=f32)
                term = jnp.concatenate([term[(m - j) % 4 * 8 : (m - j) % 4 * 8 + 8] for m in range(4)], axis=0)
                total = term if total is None else total + term
            new.append(total)
        key, value = new
    else:
        width = gain.shape[1]
        scale = inverse_rms(lambda c: rows_at(parts, c), rows, width)
        steps = width // CHUNK

        def step(c, totals):
            @pl.when(c == 0)
            def _():
                for copy in early:
                    copy.wait()

            @pl.when(c == steps // 2)
            def _():
                for copy in late:
                    copy.wait()

            cut = columns(c)
            normed = (rows_at(parts, c) * scale * gain[:, cut].astype(f32)).astype(bf16)
            terms = [jnp.dot(normed, vq[w, cut, :], preferred_element_type=f32) for w in range(copies_of)]
            both = vkv[:, :, :, cut].reshape(2 * HD, CHUNK)
            terms.append(lax.dot_general(normed, both, NT, preferred_element_type=f32))
            return tuple(total + term for total, term in zip(totals, terms))

        zeros = jnp.zeros((rows, 2 * HD), f32)
        totals = lax.fori_loop(0, steps, step, (zeros,) * (copies_of + 1))
        for w in range(copies_of):
            q = totals[w].astype(bf16).astype(f32)
            queries += [q[:, h * HD : (h + 1) * HD] for h in range(q.shape[1] // HD)]
        pair = totals[-1].astype(bf16).astype(f32)
        key, value = pair[:, :HD], pair[:, HD:]
    heads = len(queries)
    queries = jnp.concatenate(queries, axis=0)
    new_key = jnp.concatenate([key] * heads, axis=0)
    new_value = jnp.concatenate([value] * heads, axis=0)
    factor = HD ** (-0.5)
    own_score = jnp.sum(queries * new_key, axis=-1, keepdims=True) * factor
    k_copy.wait()
    scores = lax.dot_general(
        queries.astype(bf16), vk[...].reshape(-1, HD), NT, preferred_element_type=f32
    )
    scores = scores * factor
    at = lax.broadcasted_iota(jnp.int32, scores.shape, 1)
    live = (at >= bounds[0, :, 0:1]) & (at < bounds[1, :, 0:1])
    scores = jnp.where(live, scores, -1e30)
    peak = jnp.maximum(jnp.max(scores, axis=-1, keepdims=True), own_score)
    weights = jnp.where(live, jnp.exp(scores - peak), 0.0)
    own = jnp.exp(own_score - peak)
    whole = jnp.sum(weights, axis=-1, keepdims=True) + own
    weights = (weights / whole).astype(bf16)
    own = (own / whole).astype(bf16).astype(f32)
    v_copy.wait()
    mixed = jnp.dot(weights, vv[...].reshape(-1, HD), preferred_element_type=f32)
    mixed = mixed + own * new_value
    per = heads // copies_of
    mixed = [
        jnp.concatenate(
            [mixed[(w * per + h) * rows : (w * per + h + 1) * rows] for h in range(per)], axis=1
        ).astype(bf16)
        for w in range(copies_of)
    ]
    for copy in sum(o_copies, []):
        copy.wait()

    def emit(c, nothing):
        cut = columns(c)
        total = jnp.dot(mixed[0], vo[0, :, cut], preferred_element_type=f32)
        for w in range(1, copies_of):
            total = total + jnp.dot(mixed[w], vo[w, :, cut], preferred_element_type=f32)
        for j in range(blocks):
            outs[j][:, cut] = total[8 * j : 8 * j + 8].astype(bf16)
        return nothing

    lax.fori_loop(0, outs[0].shape[1] // CHUNK, emit, 0)


def attention(place, parts, gain, bounds, wq, wo, wkv, cache, given=None):
    copies_of, ready = len(wo), given is not None
    blocks = 4 if ready else len(parts)
    width = wo[0][0].shape[1]
    ctx, hd = cache.shape[4:]
    kv_rows = (2, 16) if blocks == 4 else (1, 8)
    flat_o, counts = lay_out(wo)
    shape_o = (copies_of, sum(x.shape[0] for x in wo[0]), width)
    if ready:
        early = [*given, bounds]
        late = [*flat_o, cache]
        scratch = []
    else:
        flat_q, _ = lay_out(wq)
        early = [*parts, gain, bounds]
        late = [*flat_q, *flat_o, *wkv, cache]
        scratch = [
            pltpu.VMEM((copies_of, sum(x.shape[0] for x in wq[0]), wq[0][0].shape[1]), bf16),
            pltpu.VMEM((2, 4, HD // 4, width), bf16),
        ]
    return pl.pallas_call(
        lambda *refs: attention_kernel(blocks, copies_of, counts, ready, *refs),
        in_specs=[smem_spec()] + [vmem_spec()] * len(early) + [any_spec()] * len(late),
        out_specs=[vmem_spec()] * blocks,
        out_shape=[jax.ShapeDtypeStruct((8, width), bf16)] * blocks,
        scratch_shapes=scratch
        + [
            pltpu.VMEM(shape_o, bf16),
            pltpu.VMEM(kv_rows + (ctx, hd), bf16),
            pltpu.VMEM(kv_rows + (ctx, hd), bf16),
            pltpu.SemaphoreType.DMA((8 * SPLIT + 10,)),
        ],
        compiler_params=pltpu.CompilerParams(vmem_limit_bytes=36 * MIB),
        name="attention",
    )(place, *early, *late)


def middle_kernel(state, first, second, third, fourth, gain, residual, entry):
    total = state[...].astype(f32)
    for part in (first, second, third, fourth):
        total = total + part[...].astype(f32)
    residual[...] = total
    scale = lax.rsqrt(jnp.mean(total * total, axis=-1, keepdims=True) + NORM_EPSILON)
    entry[...] = (total * scale * gain[...].astype(f32)).astype(bf16)


def middle(state, parts, gain):
    return pl.pallas_call(
        middle_kernel,
        in_specs=[vmem_spec()] * 6,
        out_specs=[vmem_spec()] * 2,
        out_shape=[jax.ShapeDtypeStruct(state.shape, f32), jax.ShapeDtypeStruct(state.shape, bf16)],
        compiler_params=pltpu.CompilerParams(vmem_limit_bytes=8 * MIB),
        name="middle",
    )(state, *parts, gain)


def expert_kernel(blocks, copies_of, counts, fused, place, *refs):
    take = Taker(refs)
    if fused:
        inputs = take(6)
    else:
        parts = take(blocks)
    router, chosen = take(2)
    weights = [take(n) for n in counts]
    outs = take(blocks)
    if fused:
        (residual,) = take(1)
    vw, sems = take(2)
    if fused:
        parts = take(1)
    units = vw.shape[1] // 3
    copies = [piece_copies(weights[w], vw.at[w], sems, w, ROW_SPLIT) for w in range(copies_of)]
    inner = ROW_SPLIT * 2 // 3
    early = sum([some[:inner] for some in copies], [])
    late = sum([some[inner:] for some in copies], [])
    for copy in early + late:
        copy.start()
    rows, width = 8 * blocks, router.shape[1]
    if fused:
        middle_kernel(*inputs, residual, parts[0])
    for copy in early:
        copy.wait()

    def step(c, totals):
        cut = columns(c)
        wide = rows_at(parts, c)
        entry = wide.astype(bf16)
        logits = [totals[i] + wide * router[i : i + 1, cut].astype(f32) for i in range(EXPS)]
        terms = [
            totals[EXPS + w]
            + lax.dot_general(entry, vw[w, 0 : 2 * units, cut], NT, preferred_element_type=f32)
            for w in range(copies_of)
        ]
        return tuple(logits + terms)

    zeros = (jnp.zeros((rows, CHUNK), f32),) * EXPS + (jnp.zeros((rows, 2 * units), f32),) * copies_of
    totals = lax.fori_loop(0, width // CHUNK, step, zeros)
    first = jnp.sum(totals[0], axis=-1, keepdims=True)
    second = jnp.sum(totals[1], axis=-1, keepdims=True)
    peak = jnp.maximum(first, second)
    first = jnp.exp(first - peak)
    second = jnp.exp(second - peak)
    expert = place[2]
    prob = jnp.where(expert == 0, first, second) / (first + second)
    mine = jnp.where(chosen[:, 0:1] == expert, prob, 0.0)
    hidden = []
    for w in range(copies_of):
        gate, upper = totals[EXPS + w][:, :units], totals[EXPS + w][:, units:]
        hidden.append((gate * jax.nn.sigmoid(gate) * upper).astype(bf16))
    for copy in late:
        copy.wait()

    def emit(c, nothing):
        cut = columns(c)
        total = jnp.dot(hidden[0], vw[0, 2 * units :, cut], preferred_element_type=f32)
        for w in range(1, copies_of):
            total = total + jnp.dot(hidden[w], vw[w, 2 * units :, cut], preferred_element_type=f32)
        total = total * mine
        for j in range(blocks):
            outs[j][:, cut] = total[8 * j : 8 * j + 8].astype(bf16)
        return nothing

    lax.fori_loop(0, width // CHUNK, emit, 0)


def experts(place, parts, router, chosen, weights, fused=None):
    blocks, copies_of = 1 if fused else len(parts), len(weights)
    flat, counts = lay_out(weights)
    width = flat[0].shape[1]
    total = sum(x.shape[0] for x in weights[0])
    early = fused or parts
    outs = [jax.ShapeDtypeStruct((8, width), bf16)] * blocks
    scratch = [
        pltpu.VMEM((copies_of, total, width), bf16),
        pltpu.SemaphoreType.DMA((ROW_SPLIT * copies_of,)),
    ]
    if fused:
        outs.append(jax.ShapeDtypeStruct((8, width), f32))
        scratch.append(pltpu.VMEM((8, width), bf16))
    return pl.pallas_call(
        lambda *refs: expert_kernel(blocks, copies_of, counts, bool(fused), *refs),
        in_specs=[smem_spec()] + [vmem_spec()] * (len(early) + 2) + [any_spec()] * len(flat),
        out_specs=[vmem_spec()] * len(outs),
        out_shape=outs,
        scratch_shapes=scratch,
        compiler_params=pltpu.CompilerParams(vmem_limit_bytes=36 * MIB),
        name="experts",
    )(place, *early, router, chosen, *flat)


def blank_kernel(*refs):
    pass


def blank(shapes):
    return pl.pallas_call(
        blank_kernel,
        out_specs=[any_spec()] * len(shapes),
        out_shape=[jax.ShapeDtypeStruct(shape, bf16) for shape in shapes],
        name="blank",
    )()


def sum_parts(parts):
    total = parts[0].astype(f32)
    for part in parts[1:]:
        total = total + part.astype(f32)
    return total


def gather_z(block):
    return [block] + [send(block, lambda s, x, z, k=k: (s, x, z + k)) for k in (1, 2, 3)]


def scatter_z(blocks):
    return sum_parts(
        [blocks[0]] + [send(blocks[j], lambda s, x, z, j=j: (s, x, z - j)) for j in (2, 1, 3)]
    ).astype(bf16)


def around_x(block):
    return [block] + [send(block, lambda s, x, z, k=k: (s, x + k, z)) for k in (2, 1, 3)]


def local(
    fresh_rows,
    row_bounds,
    layer_section,
    rows_in,
    attn_norm,
    q_proj,
    kv_proj,
    o_proj,
    kv_cache,
    cache_lengths,
    moe_norm,
    router,
    expert_ids,
):
    sections = lax.axis_size("section")
    shards = lax.axis_size("shard")
    section_pos = lax.axis_index("section")
    shard_pos = lax.axis_index("shard")
    x_pos = shard_pos // 4
    z_pos = shard_pos % 4
    width = rows_in.shape[2]

    pieces = fresh_rows[0, 0]
    layer_ids = jnp.arange(layer_section.shape[0], dtype=jnp.int32)
    order = jnp.sum(
        jnp.where(layer_section[None, :] == layer_ids[:, None], layer_ids[None, :], 0), axis=1
    ).astype(jnp.int32)
    owner = section_pos * shards + shard_pos
    base = (PIECE * owner).astype(jnp.int32)
    starts = lax.dynamic_slice_in_dim(row_bounds, owner, 1, 1)[:, 0]
    ends = lax.dynamic_slice_in_dim(row_bounds, owner + 1, 1, 1)[:, 0]
    slot = jnp.arange(pieces.shape[1], dtype=jnp.int32)[None, None, :]
    edge = jnp.arange(EDGE, dtype=jnp.int32)[None, :, None]
    pick = (slot == edge + (base + PIECE - starts)[:, None, None]).astype(bf16)
    count = sections * shards
    up = [(i, (i + 1) % count) for i in range(count)]
    down = [((i + 1) % count, i) for i in range(count)]

    to_right = jnp.einsum("lts,lsd->ltd", pick, pieces, preferred_element_type=f32).astype(bf16)
    from_left = lax.ppermute(to_right, AXES, up)
    from_right = lax.ppermute(pieces[:, :EDGE], AXES, down)

    micro, batch, _ = rows_in.shape
    rows = micro * batch
    heads_dev = q_proj.shape[2] // HD
    ctx = kv_cache.shape[5]
    shared_head = shard_pos * heads_dev // (HEADS // KVH)
    expert_pos = shard_pos // (shards // EXPS)
    place = jnp.stack([shared_head, z_pos, expert_pos, x_pos]).astype(jnp.int32)
    block_at = (z_pos - jnp.arange(4, dtype=jnp.int32)) % 4
    row_at = (block_at[:, None] * 8 + jnp.arange(8, dtype=jnp.int32)[None, :]).reshape(rows)
    lengths = jnp.take(cache_lengths.reshape(rows), row_at)
    low = row_at * ctx
    wide = (2, heads_dev, rows, HD)
    bounds = jnp.broadcast_to(jnp.stack((low, low + lengths))[:, None, :, None], wide).reshape(2, -1, HD)
    own_low = jnp.arange(8, dtype=jnp.int32) * ctx
    wide = (2, 4 * heads_dev, 8, HD)
    own_bounds = jnp.broadcast_to(
        jnp.stack((own_low, own_low + lengths[:8]))[:, None, :, None], wide
    ).reshape(2, -1, HD)
    router_rows = router[0].T
    chosen = jnp.broadcast_to(jnp.take(expert_ids[0].reshape(rows), row_at)[:, None], (rows, HD))
    entry_rows = rows_in.reshape(rows, width)
    entry_blocks = [lax.dynamic_slice_in_dim(entry_rows, 8 * block_at[j], 8, 0) for j in range(4)]
    own_kv = kv_proj[0].T
    shift = {0: 1, 1: 2, 2: 0, 3: 3}
    cross = {0: 0, 1: 3, 2: 1, 3: 2}

    def key_value(own):
        pair_a = send(own, lambda s, x, z: (s, shift[x], z))
        pair_b = send(own, lambda s, x, z: (s, cross[x], z))
        keys = jnp.where(x_pos == 0, own, jnp.where(x_pos == 3, pair_b, pair_a))
        values = jnp.where(x_pos == 0, pair_a, jnp.where(x_pos == 3, own, pair_b))
        return jnp.stack((keys, values), axis=0)

    def first_attention(state):
        q, pair = project(place, entry_blocks, attn_norm, q_proj[0], own_kv)
        pairs = gather_z(key_value(pair))
        blocks = attention(
            place, None, None, bounds, None, [[o_proj[0]]], None, kv_cache[0], given=[q, *pairs]
        )
        return middle(state, around_x(scatter_z(blocks)), moe_norm)

    (entry_blocks, own_kv, bounds, own_bounds, chosen, router_rows, place, from_left) = lax.optimization_barrier(
        (entry_blocks, own_kv, bounds, own_bounds, chosen, router_rows, place, from_left)
    )
    shares = build_shares(order, starts, ends, base[None], pieces, from_left, from_right)
    arrived = lax.all_to_all(shares, "section", split_axis=0, concat_axis=0, tiled=True)
    dest_rows = arrived.reshape(sections * PIECE, width)
    state, _ = lax.optimization_barrier((entry_blocks[0], shares))
    residual, entry = lax.cond(
        section_pos == 0, first_attention, lambda state: (state.astype(f32), state), state
    )

    q_own, o_own = q_proj[0], o_proj[0]

    def ring_copies(own):
        half = own.shape[0] // 2
        behind = send(own, lambda s, x, z: (s, x, z + 1))
        ahead = send(own, lambda s, x, z: (s, x, z - 1))
        far_a = send(behind[:half], lambda s, x, z: (s, x, z + 1))
        far_b = send(ahead[half:], lambda s, x, z: (s, x, z - 1))
        return behind, ahead, far_a, far_b

    def ring_shapes(own):
        half = (own.shape[0] // 2, own.shape[1])
        return [own.shape, own.shape, half, half]

    def with_own(own, copies):
        behind, ahead, far_a, far_b = copies
        return [[own], [behind], [ahead], [far_a, far_b]]

    copy_shapes = ring_shapes(q_own) + ring_shapes(o_own)

    def pair_only(own_kv):
        return (*gather_z(key_value(own_kv)), *blank(copy_shapes))

    def with_copies(own_kv):
        return (*gather_z(key_value(own_kv)), *ring_copies(q_own), *ring_copies(o_own))

    def no_copies(own_kv):
        return tuple(blank([(2,) + own_kv.shape] * 4 + copy_shapes))

    def among(places):
        return sum([(section_pos == place).astype(jnp.int32) for place in places])

    own_kv, _ = lax.optimization_barrier((own_kv, entry))
    copies = lax.switch(
        among(range(1, sections)) + among(RING_ATTENTION), [no_copies, pair_only, with_copies], own_kv
    )
    pair_weight = copies[:4]
    q_ring, o_ring = with_own(q_own, copies[4:8]), with_own(o_own, copies[8:])

    def first_experts(residual, entry, rows):
        blocks = experts(place, gather_z(entry), router_rows, chosen, [[rows]])
        state = sum_parts([residual] + around_x(scatter_z(blocks))).astype(bf16)
        return (state, *quantize(rows))

    def no_experts(residual, entry, rows):
        return (*blank([(8, width)]), *quantize(rows))

    entry, _ = lax.optimization_barrier((entry, pair_weight))
    state, coded, scale = lax.cond(section_pos == 0, first_experts, no_experts, residual, entry, dest_rows)
    keep = state
    source, _ = lax.optimization_barrier((dest_rows, state))
    copies = lax.cond(
        among([tick for tick in RING_EXPERTS if tick < sections - 1]) == 1,
        lambda rows: ring_copies(rows),
        lambda rows: tuple(blank(ring_shapes(dest_rows))),
        source,
    )
    state, copies = lax.optimization_barrier((state, copies))
    rows_ring = with_own(dest_rows, copies)

    def hop(tick):
        count = 1 if tick in RING_ATTENTION else 4

        def move(s, x, z, k):
            return ((s ^ 1) if tick % 2 else (s - 1 if s % 2 == 0 else s + 1), x, z + k)

        def run(state):
            return tuple(send(state, lambda s, x, z, k=k: move(s, x, z, k)) for k in range(count))

        return run

    def layer(tick, rows_ring):
        def run(*blocks):
            state = blocks[0]
            if tick in RING_ATTENTION:
                summed = attention(
                    place, [state], attn_norm, own_bounds, q_ring, o_ring, pair_weight, kv_cache[0]
                )[0]
            else:
                summed = scatter_z(
                    attention(
                        place, blocks, attn_norm, bounds, [[q_own]], [[o_own]], pair_weight, kv_cache[0]
                    )
                )
            if tick in RING_EXPERTS:
                summed, residual = experts(
                    place, None, router_rows, chosen[:8], rows_ring, fused=[state, *around_x(summed), moe_norm]
                )
            else:
                residual, entry = middle(state, around_x(summed), moe_norm)
                summed = scatter_z(experts(place, gather_z(entry), router_rows, chosen, [[dest_rows]]))
            return sum_parts([residual] + around_x(summed)).astype(bf16)

        return run

    def nothing(count):
        def run(*_):
            return tuple(blank([(8, width)] * count))

        return run

    def hop_to(tick, state):
        step = hop(tick)
        count = 1 if tick in RING_ATTENTION else 4
        return lax.cond(
            (section_pos == tick - 1) | (section_pos == tick), step, nothing(count), state
        )

    def at_layer(tick, blocks, rows_ring):
        step = layer(tick, rows_ring)
        return lax.cond(section_pos == tick, lambda *blocks: (step(*blocks),), nothing(1), *blocks)[0]

    state = at_layer(1, hop_to(1, state), rows_ring)
    keep = jnp.where(section_pos == 1, state, keep)
    for even in range(2, sections, 2):
        blocks = hop_to(even, state)
        here = (section_pos == even) | (section_pos == even + 1)

        def pair(*blocks, even=even):
            ring = rows_ring
            if even + 2 == sections:
                copies = lax.cond(
                    section_pos == even + 1,
                    lambda rows: ring_copies(rows),
                    lambda rows: tuple(blank(ring_shapes(dest_rows))),
                    dest_rows,
                )
                blocks, copies = lax.optimization_barrier((blocks, copies))
                ring = with_own(dest_rows, copies)
            first = at_layer(even, blocks, rows_ring)
            second = at_layer(even + 1, hop(even + 1)(first), ring)
            return (jnp.where(section_pos == even, first, second),)

        (state,) = lax.cond(here, pair, nothing(1), *blocks)
        keep = jnp.where(here, state, keep)
    blocks = gather_z(keep)
    whole = jnp.concatenate(blocks, axis=0)
    wanted = jnp.arange(micro, dtype=jnp.int32) * batch + shard_pos
    found = jnp.argmax(row_at[None, :] == wanted[:, None], axis=1)
    outputs = jnp.take(whole, found, axis=0)
    return (coded[None, None], scale[None, None], outputs[None, :, None])


def solution(mesh):
    return jax.shard_map(
        local,
        mesh=mesh,
        in_specs=(
            P("section", "shard", None, None, None),
            P(),
            P(),
            P(),
            P("section", None),
            P("section", None, "shard"),
            P("section", None, "shard"),
            P("section", "shard", None),
            P("section", None, None, None, None, None, None),
            P(),
            P("section", None),
            P("section", None, None),
            P("section", None, None),
        ),
        out_specs=(
            P("section", "shard", None, None),
            P("section", "shard", None, None),
            P("section", None, "shard", None),
        ),
        check_vma=False,
    )
```

```python
import jax
import jax.numpy as jnp
from jax import lax
from jax.experimental import pallas as pl
from jax.experimental.pallas import tpu as pltpu
from jax.sharding import PartitionSpec as P

HD = 128
HEADS = 32
KVH = 2
EXPS = 2
QB = 128
EDGE = 8
PIECE = 48
CODE_LIMIT = 448.0
NORM_EPSILON = 1e-06
MIB = 1024 * 1024
RING_ATTENTION = (3, 4, 5, 6, 7)
RING_EXPERTS = (3, 5, 6, 7)

bf16 = jnp.bfloat16
f32 = jnp.float32
NT = (((1,), (1,)), ((), ()))


def pairs_of(move):
    result = []
    for s in range(8):
        for x in range(4):
            for z in range(4):
                s2, x2, z2 = move(s, x, z)
                result.append((s * 16 + x * 4 + z, s2 % 8 * 16 + x2 % 4 * 4 + z2 % 4))
    return result


AXES = ("section", "shard")


def send(value, move):
    return lax.ppermute(value, AXES, pairs_of(move))


def share_kernel(order, starts, ends, base, piece_ref, left_ref, right_ref, out_ref):
    layer = order[pl.program_id(0)]
    first = starts[layer] - base[0]
    stop = ends[layer] - base[0]
    t = lax.broadcasted_iota(jnp.int32, (PIECE, 64), 0)
    r = lax.broadcasted_iota(jnp.int32, (PIECE, 64), 1)
    own = jnp.where((r == t - first) & (t < stop), 1.0, 0.0).astype(bf16)
    t = lax.broadcasted_iota(jnp.int32, (PIECE, 16), 0)
    r = lax.broadcasted_iota(jnp.int32, (PIECE, 16), 1)
    near = (r < EDGE) & (r == t) & (t < first)
    far = (r >= EDGE) & (r - EDGE == t - stop) & (t >= stop)
    rim = jnp.where(near | far, 1.0, 0.0).astype(bf16)

    rims = jnp.concatenate((left_ref[0].astype(f32), right_ref[0].astype(f32)), axis=0).astype(bf16)
    total = jnp.dot(own, piece_ref[0], preferred_element_type=f32)
    total = total + jnp.dot(rim, rims, preferred_element_type=f32)
    out_ref[0] = total.astype(bf16)


def build_shares(order, starts, ends, base, pieces, from_left, from_right):
    layers, slots, width = pieces.shape
    return pl.pallas_call(
        share_kernel,
        grid_spec=pltpu.PrefetchScalarGridSpec(
            num_scalar_prefetch=4,
            grid=(layers,),
            in_specs=[
                pl.BlockSpec((1, slots, width), lambda d, o, *_: (o[d], 0, 0)),
                pl.BlockSpec((1, EDGE, width), lambda d, o, *_: (o[d], 0, 0)),
                pl.BlockSpec((1, EDGE, width), lambda d, o, *_: (o[d], 0, 0)),
            ],
            out_specs=pl.BlockSpec((1, PIECE, width), lambda d, *_: (d, 0, 0)),
        ),
        out_shape=jax.ShapeDtypeStruct((layers, PIECE, width), bf16),
        compiler_params=pltpu.CompilerParams(vmem_limit_bytes=24 * MIB),
        name="build_shares",
    )(order, starts, ends, base, pieces, from_left, from_right)


def quantize_kernel(rows_ref, coded_ref, scale_ref):
    step = pl.program_id(0)
    rows, width = rows_ref.shape
    cols = width // QB
    at_r = lax.broadcasted_iota(jnp.int32, scale_ref.shape, 0)
    at_c = lax.broadcasted_iota(jnp.int32, scale_ref.shape, 1)
    scales = jnp.where(step == 0, jnp.zeros(scale_ref.shape, f32), scale_ref[...])

    for c in range(cols):
        at = slice(c * QB, (c + 1) * QB)
        for i in range(rows // QB):
            tile = rows_ref[i * QB : (i + 1) * QB, at].astype(f32)
            peak = jnp.max(jnp.max(jnp.abs(tile), axis=0, keepdims=True), axis=1, keepdims=True)
            scale = (peak + 1e-06) / CODE_LIMIT
            coded_ref[i * QB : (i + 1) * QB, at] = (tile * (1.0 / scale)).astype(bf16)
            scales = jnp.where((at_r == i) & (at_c == step * cols + c), scale, scales)
    scale_ref[...] = scales


def quantize(rows):
    count, width = rows.shape
    chunk = 1024
    return pl.pallas_call(
        quantize_kernel,
        grid=(width // chunk,),
        in_specs=[pl.BlockSpec((count, chunk), lambda i: (0, i))],
        out_specs=[
            pl.BlockSpec((count, chunk), lambda i: (0, i)),
            pl.BlockSpec((count // QB, width // QB), lambda i: (0, 0)),
        ],
        out_shape=[
            jax.ShapeDtypeStruct((count, width), bf16),
            jax.ShapeDtypeStruct((count // QB, width // QB), f32),
        ],
        compiler_params=pltpu.CompilerParams(vmem_limit_bytes=24 * MIB),
        name="quantize",
    )(rows)


CHUNK = 2048


def rows_at(refs, c):
    at = pl.ds(pl.multiple_of(c * CHUNK, CHUNK), CHUNK)
    return jnp.concatenate([ref[:, at].astype(f32) for ref in refs], axis=0)


def columns(c):
    return pl.ds(pl.multiple_of(c * CHUNK, CHUNK), CHUNK)


def inverse_rms(load, rows, width):
    def add(c, total):
        wide = load(c)
        return total + wide * wide

    total = lax.fori_loop(0, width // CHUNK, add, jnp.zeros((rows, CHUNK), f32))
    return lax.rsqrt(jnp.sum(total, axis=-1, keepdims=True) / width + NORM_EPSILON)


def any_spec():
    return pl.BlockSpec(memory_space=pltpu.HBM)


def smem_spec():
    return pl.BlockSpec(memory_space=pltpu.SMEM)


def vmem_spec():
    return pl.BlockSpec(memory_space=pltpu.VMEM)


SPLIT = 4
ROW_SPLIT = 6


def piece_copies(pieces, target, sems, first, split=SPLIT):
    copies, at = [], 0
    parts = split // len(pieces)
    for i, piece in enumerate(pieces):
        size = piece.shape[0] // parts
        for j in range(parts):
            copies.append(
                pltpu.make_async_copy(
                    piece.at[pl.ds(j * size, size)],
                    target.at[pl.ds(at, size)],
                    sems.at[first * split + i * parts + j],
                )
            )
            at += size
    return copies


class Taker:
    def __init__(self, refs):
        self.refs = list(refs)

    def __call__(self, count):
        result = self.refs[:count]
        del self.refs[:count]
        return result


def lay_out(lists):
    return [x for pieces in lists for x in pieces], [len(pieces) for pieces in lists]


def project_kernel(place, *refs):
    take = Taker(refs)
    parts = take(4)
    gain, wq, wkv, q, pair, vq, sem = take(7)
    del place
    copies = piece_copies([wq], vq, sem, 0)
    for copy in copies:
        copy.start()
    rows, width = 8 * len(parts), gain.shape[1]
    scale = inverse_rms(lambda c: rows_at(parts, c), rows, width)
    for copy in copies:
        copy.wait()

    def step(c, totals):
        at = columns(c)
        normed = (rows_at(parts, c) * scale * gain[:, at].astype(f32)).astype(bf16)
        return (
            totals[0] + jnp.dot(normed, vq[at, :], preferred_element_type=f32),
            totals[1] + lax.dot_general(normed, wkv[:, at], NT, preferred_element_type=f32),
        )

    zeros = (jnp.zeros(q.shape, f32), jnp.zeros(pair.shape, f32))
    totals = lax.fori_loop(0, width // CHUNK, step, zeros)
    q[...] = totals[0].astype(bf16)
    pair[...] = totals[1].astype(bf16)


def project(place, parts, gain, wq, wkv):
    rows = 8 * len(parts)
    return pl.pallas_call(
        project_kernel,
        in_specs=[smem_spec()] + [vmem_spec()] * 5 + [any_spec(), vmem_spec()],
        out_specs=[vmem_spec()] * 2,
        out_shape=[
            jax.ShapeDtypeStruct((rows, wq.shape[1]), bf16),
            jax.ShapeDtypeStruct((rows, wkv.shape[0]), bf16),
        ],
        scratch_shapes=[pltpu.VMEM(wq.shape, bf16), pltpu.SemaphoreType.DMA((SPLIT,))],
        compiler_params=pltpu.CompilerParams(vmem_limit_bytes=16 * MIB),
        name="project",
    )(place, *parts, gain, wq, wkv)


def attention_kernel(blocks, copies_of, counts, ready, place, *refs):
    take = Taker(refs)
    if ready:
        (q_ref,) = take(1)
        pairs = take(4)
        (bounds,) = take(1)
    else:
        parts = take(blocks)
        gain, bounds = take(2)
        wq = [take(n) for n in counts]
    wo = [take(n) for n in counts]
    if not ready:
        wkv = take(4)
    (cache,) = take(1)
    outs = take(blocks)
    if not ready:
        vq, vkv = take(2)
    vo, vk, vv, sems = take(4)
    head, z = place[0], place[1]
    rows = 8 * blocks
    q_copies, kv_copies = [], []
    if not ready:
        q_copies = [piece_copies(wq[w], vq.at[w], sems, w) for w in range(copies_of)]
        kv_copies = [
            pltpu.make_async_copy(wkv[j].at[p], vkv.at[p, (z + 4 - j) % 4], sems.at[8 * SPLIT + 4 * p + j])
            for p in range(2)
            for j in range(4)
        ]
    if blocks == 4:
        k_copy = pltpu.make_async_copy(cache.at[:, :, 0, head], vk, sems.at[8 * SPLIT + 8])
        v_copy = pltpu.make_async_copy(cache.at[:, :, 1, head], vv, sems.at[8 * SPLIT + 9])
    else:
        own = pl.ds((z % 2) * 8, 8)
        k_copy = pltpu.make_async_copy(cache.at[z // 2, own, 0, head], vk.at[0], sems.at[8 * SPLIT + 8])
        v_copy = pltpu.make_async_copy(cache.at[z // 2, own, 1, head], vv.at[0], sems.at[8 * SPLIT + 9])
    o_copies = [piece_copies(wo[w], vo.at[w], sems, 4 + w) for w in range(copies_of)]
    half = SPLIT // 2
    early = sum([copies[:half] for copies in q_copies], []) + kv_copies
    late = sum([copies[half:] for copies in q_copies], [])
    for copy in early + late + [k_copy, v_copy] + sum(o_copies, []):
        copy.start()
    queries = []
    if ready:
        q = q_ref[...].astype(f32)
        queries = [q[:, h * HD : (h + 1) * HD] for h in range(q.shape[1] // HD)]
        new = []
        for p in range(2):
            total = None
            for j in range(4):
                at_r = lax.broadcasted_iota(jnp.int32, (HD // 4, HD), 0)
                at_c = lax.broadcasted_iota(jnp.int32, (HD // 4, HD), 1)
                spot = jnp.where(at_c == (z + 4 - j) % 4 * (HD // 4) + at_r, 1.0, 0.0).astype(bf16)
                term = jnp.dot(pairs[j][p], spot, preferred_element_type=f32)
                term = jnp.concatenate([term[(m - j) % 4 * 8 : (m - j) % 4 * 8 + 8] for m in range(4)], axis=0)
                total = term if total is None else total + term
            new.append(total)
        key, value = new
    else:
        width = gain.shape[1]
        scale = inverse_rms(lambda c: rows_at(parts, c), rows, width)
        steps = width // CHUNK

        def step(c, totals):
            @pl.when(c == 0)
            def _():
                for copy in early:
                    copy.wait()

            @pl.when(c == steps // 2)
            def _():
                for copy in late:
                    copy.wait()

            cut = columns(c)
            normed = (rows_at(parts, c) * scale * gain[:, cut].astype(f32)).astype(bf16)
            terms = [jnp.dot(normed, vq[w, cut, :], preferred_element_type=f32) for w in range(copies_of)]
            both = vkv[:, :, :, cut].reshape(2 * HD, CHUNK)
            terms.append(lax.dot_general(normed, both, NT, preferred_element_type=f32))
            return tuple(total + term for total, term in zip(totals, terms))

        zeros = jnp.zeros((rows, 2 * HD), f32)
        totals = lax.fori_loop(0, steps, step, (zeros,) * (copies_of + 1))
        for w in range(copies_of):
            q = totals[w].astype(bf16).astype(f32)
            queries += [q[:, h * HD : (h + 1) * HD] for h in range(q.shape[1] // HD)]
        pair = totals[-1].astype(bf16).astype(f32)
        key, value = pair[:, :HD], pair[:, HD:]
    heads = len(queries)
    queries = jnp.concatenate(queries, axis=0)
    new_key = jnp.concatenate([key] * heads, axis=0)
    new_value = jnp.concatenate([value] * heads, axis=0)
    factor = HD ** (-0.5)
    own_score = jnp.sum(queries * new_key, axis=-1, keepdims=True) * factor
    k_copy.wait()
    scores = lax.dot_general(
        queries.astype(bf16), vk[...].reshape(-1, HD), NT, preferred_element_type=f32
    )
    scores = scores * factor
    at = lax.broadcasted_iota(jnp.int32, scores.shape, 1)
    live = (at >= bounds[0, :, 0:1]) & (at < bounds[1, :, 0:1])
    scores = jnp.where(live, scores, -1e30)
    peak = jnp.maximum(jnp.max(scores, axis=-1, keepdims=True), own_score)
    weights = jnp.where(live, jnp.exp(scores - peak), 0.0)
    own = jnp.exp(own_score - peak)
    whole = jnp.sum(weights, axis=-1, keepdims=True) + own
    weights = (weights / whole).astype(bf16)
    own = (own / whole).astype(bf16).astype(f32)
    v_copy.wait()
    mixed = jnp.dot(weights, vv[...].reshape(-1, HD), preferred_element_type=f32)
    mixed = mixed + own * new_value
    per = heads // copies_of
    mixed = [
        jnp.concatenate(
            [mixed[(w * per + h) * rows : (w * per + h + 1) * rows] for h in range(per)], axis=1
        ).astype(bf16)
        for w in range(copies_of)
    ]
    for copy in sum(o_copies, []):
        copy.wait()

    def emit(c, nothing):
        cut = columns(c)
        total = jnp.dot(mixed[0], vo[0, :, cut], preferred_element_type=f32)
        for w in range(1, copies_of):
            total = total + jnp.dot(mixed[w], vo[w, :, cut], preferred_element_type=f32)
        for j in range(blocks):
            outs[j][:, cut] = total[8 * j : 8 * j + 8].astype(bf16)
        return nothing

    lax.fori_loop(0, outs[0].shape[1] // CHUNK, emit, 0)


def attention(place, parts, gain, bounds, wq, wo, wkv, cache, given=None):
    copies_of, ready = len(wo), given is not None
    blocks = 4 if ready else len(parts)
    width = wo[0][0].shape[1]
    ctx, hd = cache.shape[4:]
    kv_rows = (2, 16) if blocks == 4 else (1, 8)
    flat_o, counts = lay_out(wo)
    shape_o = (copies_of, sum(x.shape[0] for x in wo[0]), width)
    if ready:
        early = [*given, bounds]
        late = [*flat_o, cache]
        scratch = []
    else:
        flat_q, _ = lay_out(wq)
        early = [*parts, gain, bounds]
        late = [*flat_q, *flat_o, *wkv, cache]
        scratch = [
            pltpu.VMEM((copies_of, sum(x.shape[0] for x in wq[0]), wq[0][0].shape[1]), bf16),
            pltpu.VMEM((2, 4, HD // 4, width), bf16),
        ]
    return pl.pallas_call(
        lambda *refs: attention_kernel(blocks, copies_of, counts, ready, *refs),
        in_specs=[smem_spec()] + [vmem_spec()] * len(early) + [any_spec()] * len(late),
        out_specs=[vmem_spec()] * blocks,
        out_shape=[jax.ShapeDtypeStruct((8, width), bf16)] * blocks,
        scratch_shapes=scratch
        + [
            pltpu.VMEM(shape_o, bf16),
            pltpu.VMEM(kv_rows + (ctx, hd), bf16),
            pltpu.VMEM(kv_rows + (ctx, hd), bf16),
            pltpu.SemaphoreType.DMA((8 * SPLIT + 10,)),
        ],
        compiler_params=pltpu.CompilerParams(vmem_limit_bytes=36 * MIB),
        name="attention",
    )(place, *early, *late)


def middle_kernel(state, first, second, third, fourth, gain, residual, entry):
    total = state[...].astype(f32)
    for part in (first, second, third, fourth):
        total = total + part[...].astype(f32)
    residual[...] = total
    scale = lax.rsqrt(jnp.mean(total * total, axis=-1, keepdims=True) + NORM_EPSILON)
    entry[...] = (total * scale * gain[...].astype(f32)).astype(bf16)


def middle(state, parts, gain):
    return pl.pallas_call(
        middle_kernel,
        in_specs=[vmem_spec()] * 6,
        out_specs=[vmem_spec()] * 2,
        out_shape=[jax.ShapeDtypeStruct(state.shape, f32), jax.ShapeDtypeStruct(state.shape, bf16)],
        compiler_params=pltpu.CompilerParams(vmem_limit_bytes=8 * MIB),
        name="middle",
    )(state, *parts, gain)


def expert_kernel(blocks, copies_of, counts, fused, place, *refs):
    take = Taker(refs)
    if fused:
        inputs = take(6)
    else:
        parts = take(blocks)
    router, chosen = take(2)
    weights = [take(n) for n in counts]
    outs = take(blocks)
    if fused:
        (residual,) = take(1)
    vw, sems = take(2)
    if fused:
        parts = take(1)
    units = vw.shape[1] // 3
    copies = [piece_copies(weights[w], vw.at[w], sems, w, ROW_SPLIT) for w in range(copies_of)]
    inner = ROW_SPLIT * 2 // 3
    early = sum([some[:inner] for some in copies], [])
    late = sum([some[inner:] for some in copies], [])
    for copy in early + late:
        copy.start()
    rows, width = 8 * blocks, router.shape[1]
    if fused:
        middle_kernel(*inputs, residual, parts[0])
    for copy in early:
        copy.wait()

    def step(c, totals):
        cut = columns(c)
        wide = rows_at(parts, c)
        entry = wide.astype(bf16)
        logits = [totals[i] + wide * router[i : i + 1, cut].astype(f32) for i in range(EXPS)]
        terms = [
            totals[EXPS + w]
            + lax.dot_general(entry, vw[w, 0 : 2 * units, cut], NT, preferred_element_type=f32)
            for w in range(copies_of)
        ]
        return tuple(logits + terms)

    zeros = (jnp.zeros((rows, CHUNK), f32),) * EXPS + (jnp.zeros((rows, 2 * units), f32),) * copies_of
    totals = lax.fori_loop(0, width // CHUNK, step, zeros)
    first = jnp.sum(totals[0], axis=-1, keepdims=True)
    second = jnp.sum(totals[1], axis=-1, keepdims=True)
    peak = jnp.maximum(first, second)
    first = jnp.exp(first - peak)
    second = jnp.exp(second - peak)
    expert = place[2]
    prob = jnp.where(expert == 0, first, second) / (first + second)
    mine = jnp.where(chosen[:, 0:1] == expert, prob, 0.0)
    hidden = []
    for w in range(copies_of):
        gate, upper = totals[EXPS + w][:, :units], totals[EXPS + w][:, units:]
        hidden.append((gate * jax.nn.sigmoid(gate) * upper).astype(bf16))
    for copy in late:
        copy.wait()

    def emit(c, nothing):
        cut = columns(c)
        total = jnp.dot(hidden[0], vw[0, 2 * units :, cut], preferred_element_type=f32)
        for w in range(1, copies_of):
            total = total + jnp.dot(hidden[w], vw[w, 2 * units :, cut], preferred_element_type=f32)
        total = total * mine
        for j in range(blocks):
            outs[j][:, cut] = total[8 * j : 8 * j + 8].astype(bf16)
        return nothing

    lax.fori_loop(0, width // CHUNK, emit, 0)


def experts(place, parts, router, chosen, weights, fused=None):
    blocks, copies_of = 1 if fused else len(parts), len(weights)
    flat, counts = lay_out(weights)
    width = flat[0].shape[1]
    total = sum(x.shape[0] for x in weights[0])
    early = fused or parts
    outs = [jax.ShapeDtypeStruct((8, width), bf16)] * blocks
    scratch = [
        pltpu.VMEM((copies_of, total, width), bf16),
        pltpu.SemaphoreType.DMA((ROW_SPLIT * copies_of,)),
    ]
    if fused:
        outs.append(jax.ShapeDtypeStruct((8, width), f32))
        scratch.append(pltpu.VMEM((8, width), bf16))
    return pl.pallas_call(
        lambda *refs: expert_kernel(blocks, copies_of, counts, bool(fused), *refs),
        in_specs=[smem_spec()] + [vmem_spec()] * (len(early) + 2) + [any_spec()] * len(flat),
        out_specs=[vmem_spec()] * len(outs),
        out_shape=outs,
        scratch_shapes=scratch,
        compiler_params=pltpu.CompilerParams(vmem_limit_bytes=36 * MIB),
        name="experts",
    )(place, *early, router, chosen, *flat)


def blank_kernel(*refs):
    pass


def blank(shapes):
    return pl.pallas_call(
        blank_kernel,
        out_specs=[any_spec()] * len(shapes),
        out_shape=[jax.ShapeDtypeStruct(shape, bf16) for shape in shapes],
        name="blank",
    )()


def sum_parts(parts):
    total = parts[0].astype(f32)
    for part in parts[1:]:
        total = total + part.astype(f32)
    return total


def gather_z(block):
    return [block] + [send(block, lambda s, x, z, k=k: (s, x, z + k)) for k in (1, 2, 3)]


def scatter_z(blocks):
    return sum_parts(
        [blocks[0]] + [send(blocks[j], lambda s, x, z, j=j: (s, x, z - j)) for j in (2, 1, 3)]
    ).astype(bf16)


def around_x(block):
    return [block] + [send(block, lambda s, x, z, k=k: (s, x + k, z)) for k in (2, 1, 3)]


def local(
    fresh_rows,
    row_bounds,
    layer_section,
    rows_in,
    attn_norm,
    q_proj,
    kv_proj,
    o_proj,
    kv_cache,
    cache_lengths,
    moe_norm,
    router,
    expert_ids,
):
    sections = lax.axis_size("section")
    shards = lax.axis_size("shard")
    section_pos = lax.axis_index("section")
    shard_pos = lax.axis_index("shard")
    x_pos = shard_pos // 4
    z_pos = shard_pos % 4
    width = rows_in.shape[2]

    pieces = fresh_rows[0, 0]
    layer_ids = jnp.arange(layer_section.shape[0], dtype=jnp.int32)
    order = jnp.sum(
        jnp.where(layer_section[None, :] == layer_ids[:, None], layer_ids[None, :], 0), axis=1
    ).astype(jnp.int32)
    owner = section_pos * shards + shard_pos
    base = (PIECE * owner).astype(jnp.int32)
    starts = lax.dynamic_slice_in_dim(row_bounds, owner, 1, 1)[:, 0]
    ends = lax.dynamic_slice_in_dim(row_bounds, owner + 1, 1, 1)[:, 0]
    slot = jnp.arange(pieces.shape[1], dtype=jnp.int32)[None, None, :]
    edge = jnp.arange(EDGE, dtype=jnp.int32)[None, :, None]
    pick = (slot == edge + (base + PIECE - starts)[:, None, None]).astype(bf16)
    count = sections * shards
    up = [(i, (i + 1) % count) for i in range(count)]
    down = [((i + 1) % count, i) for i in range(count)]

    to_right = jnp.einsum("lts,lsd->ltd", pick, pieces, preferred_element_type=f32).astype(bf16)
    from_left = lax.ppermute(to_right, AXES, up)
    from_right = lax.ppermute(pieces[:, :EDGE], AXES, down)

    micro, batch, _ = rows_in.shape
    rows = micro * batch
    heads_dev = q_proj.shape[2] // HD
    ctx = kv_cache.shape[5]
    shared_head = shard_pos * heads_dev // (HEADS // KVH)
    expert_pos = shard_pos // (shards // EXPS)
    place = jnp.stack([shared_head, z_pos, expert_pos, x_pos]).astype(jnp.int32)
    block_at = (z_pos - jnp.arange(4, dtype=jnp.int32)) % 4
    row_at = (block_at[:, None] * 8 + jnp.arange(8, dtype=jnp.int32)[None, :]).reshape(rows)
    lengths = jnp.take(cache_lengths.reshape(rows), row_at)
    low = row_at * ctx
    wide = (2, heads_dev, rows, HD)
    bounds = jnp.broadcast_to(jnp.stack((low, low + lengths))[:, None, :, None], wide).reshape(2, -1, HD)
    own_low = jnp.arange(8, dtype=jnp.int32) * ctx
    wide = (2, 4 * heads_dev, 8, HD)
    own_bounds = jnp.broadcast_to(
        jnp.stack((own_low, own_low + lengths[:8]))[:, None, :, None], wide
    ).reshape(2, -1, HD)
    router_rows = router[0].T
    chosen = jnp.broadcast_to(jnp.take(expert_ids[0].reshape(rows), row_at)[:, None], (rows, HD))
    entry_rows = rows_in.reshape(rows, width)
    entry_blocks = [lax.dynamic_slice_in_dim(entry_rows, 8 * block_at[j], 8, 0) for j in range(4)]
    own_kv = kv_proj[0].T
    shift = {0: 1, 1: 2, 2: 0, 3: 3}
    cross = {0: 0, 1: 3, 2: 1, 3: 2}

    def key_value(own):
        pair_a = send(own, lambda s, x, z: (s, shift[x], z))
        pair_b = send(own, lambda s, x, z: (s, cross[x], z))
        keys = jnp.where(x_pos == 0, own, jnp.where(x_pos == 3, pair_b, pair_a))
        values = jnp.where(x_pos == 0, pair_a, jnp.where(x_pos == 3, own, pair_b))
        return jnp.stack((keys, values), axis=0)

    def first_attention(state):
        q, pair = project(place, entry_blocks, attn_norm, q_proj[0], own_kv)
        pairs = gather_z(key_value(pair))
        blocks = attention(
            place, None, None, bounds, None, [[o_proj[0]]], None, kv_cache[0], given=[q, *pairs]
        )
        return middle(state, around_x(scatter_z(blocks)), moe_norm)

    (entry_blocks, own_kv, bounds, own_bounds, chosen, router_rows, place, from_left) = lax.optimization_barrier(
        (entry_blocks, own_kv, bounds, own_bounds, chosen, router_rows, place, from_left)
    )
    shares = build_shares(order, starts, ends, base[None], pieces, from_left, from_right)
    arrived = lax.all_to_all(shares, "section", split_axis=0, concat_axis=0, tiled=True)
    dest_rows = arrived.reshape(sections * PIECE, width)
    state, _ = lax.optimization_barrier((entry_blocks[0], shares))
    residual, entry = lax.cond(
        section_pos == 0, first_attention, lambda state: (state.astype(f32), state), state
    )

    q_own, o_own = q_proj[0], o_proj[0]

    def ring_copies(own):
        half = own.shape[0] // 2
        behind = send(own, lambda s, x, z: (s, x, z + 1))
        ahead = send(own, lambda s, x, z: (s, x, z - 1))
        far_a = send(behind[:half], lambda s, x, z: (s, x, z + 1))
        far_b = send(ahead[half:], lambda s, x, z: (s, x, z - 1))
        return behind, ahead, far_a, far_b

    def ring_shapes(own):
        half = (own.shape[0] // 2, own.shape[1])
        return [own.shape, own.shape, half, half]

    def with_own(own, copies):
        behind, ahead, far_a, far_b = copies
        return [[own], [behind], [ahead], [far_a, far_b]]

    copy_shapes = ring_shapes(q_own) + ring_shapes(o_own)

    def pair_only(own_kv):
        return (*gather_z(key_value(own_kv)), *blank(copy_shapes))

    def with_copies(own_kv):
        return (*gather_z(key_value(own_kv)), *ring_copies(q_own), *ring_copies(o_own))

    def no_copies(own_kv):
        return tuple(blank([(2,) + own_kv.shape] * 4 + copy_shapes))

    def among(places):
        return sum([(section_pos == place).astype(jnp.int32) for place in places])

    own_kv, _ = lax.optimization_barrier((own_kv, entry))
    copies = lax.switch(
        among(range(1, sections)) + among(RING_ATTENTION), [no_copies, pair_only, with_copies], own_kv
    )
    pair_weight = copies[:4]
    q_ring, o_ring = with_own(q_own, copies[4:8]), with_own(o_own, copies[8:])

    def first_experts(residual, entry, rows):
        blocks = experts(place, gather_z(entry), router_rows, chosen, [[rows]])
        state = sum_parts([residual] + around_x(scatter_z(blocks))).astype(bf16)
        return (state, *quantize(rows))

    def no_experts(residual, entry, rows):
        return (*blank([(8, width)]), *quantize(rows))

    entry, _ = lax.optimization_barrier((entry, pair_weight))
    state, coded, scale = lax.cond(section_pos == 0, first_experts, no_experts, residual, entry, dest_rows)
    keep = state
    source, _ = lax.optimization_barrier((dest_rows, state))
    copies = lax.cond(
        among([tick for tick in RING_EXPERTS if tick < sections - 1]) == 1,
        lambda rows: ring_copies(rows),
        lambda rows: tuple(blank(ring_shapes(dest_rows))),
        source,
    )
    state, copies = lax.optimization_barrier((state, copies))
    rows_ring = with_own(dest_rows, copies)

    def hop(tick):
        count = 1 if tick in RING_ATTENTION else 4

        def move(s, x, z, k):
            return ((s ^ 1) if tick % 2 else (s - 1 if s % 2 == 0 else s + 1), x, z + k)

        def run(state):
            return tuple(send(state, lambda s, x, z, k=k: move(s, x, z, k)) for k in range(count))

        return run

    def layer(tick, rows_ring):
        def run(*blocks):
            state = blocks[0]
            if tick in RING_ATTENTION:
                summed = attention(
                    place, [state], attn_norm, own_bounds, q_ring, o_ring, pair_weight, kv_cache[0]
                )[0]
            else:
                summed = scatter_z(
                    attention(
                        place, blocks, attn_norm, bounds, [[q_own]], [[o_own]], pair_weight, kv_cache[0]
                    )
                )
            if tick in RING_EXPERTS:
                summed, residual = experts(
                    place, None, router_rows, chosen[:8], rows_ring, fused=[state, *around_x(summed), moe_norm]
                )
            else:
                residual, entry = middle(state, around_x(summed), moe_norm)
                summed = scatter_z(experts(place, gather_z(entry), router_rows, chosen, [[dest_rows]]))
            return sum_parts([residual] + around_x(summed)).astype(bf16)

        return run

    def nothing(count):
        def run(*_):
            return tuple(blank([(8, width)] * count))

        return run

    def hop_to(tick, state):
        step = hop(tick)
        count = 1 if tick in RING_ATTENTION else 4
        return lax.cond(
            (section_pos == tick - 1) | (section_pos == tick), step, nothing(count), state
        )

    def at_layer(tick, blocks, rows_ring):
        step = layer(tick, rows_ring)
        return lax.cond(section_pos == tick, lambda *blocks: (step(*blocks),), nothing(1), *blocks)[0]

    state = at_layer(1, hop_to(1, state), rows_ring)
    keep = jnp.where(section_pos == 1, state, keep)
    for even in range(2, sections, 2):
        blocks = hop_to(even, state)
        if even == 2:
            first = at_layer(2, blocks, rows_ring)
            keep = jnp.where(section_pos == 2, first, keep)
            state = at_layer(3, hop_to(3, first), rows_ring)
            keep = jnp.where(section_pos == 3, state, keep)
            continue
        here = (section_pos == even) | (section_pos == even + 1)

        def pair(*blocks, even=even):
            ring = rows_ring
            if even + 2 == sections:
                copies = lax.cond(
                    section_pos == even + 1,
                    lambda rows: ring_copies(rows),
                    lambda rows: tuple(blank(ring_shapes(dest_rows))),
                    dest_rows,
                )
                blocks, copies = lax.optimization_barrier((blocks, copies))
                ring = with_own(dest_rows, copies)
            first = at_layer(even, blocks, rows_ring)
            second = at_layer(even + 1, hop(even + 1)(first), ring)
            return (jnp.where(section_pos == even, first, second),)

        (state,) = lax.cond(here, pair, nothing(1), *blocks)
        keep = jnp.where(here, state, keep)
    blocks = gather_z(keep)
    whole = jnp.concatenate(blocks, axis=0)
    wanted = jnp.arange(micro, dtype=jnp.int32) * batch + shard_pos
    found = jnp.argmax(row_at[None, :] == wanted[:, None], axis=1)
    outputs = jnp.take(whole, found, axis=0)
    return (coded[None, None], scale[None, None], outputs[None, :, None])


def solution(mesh):
    return jax.shard_map(
        local,
        mesh=mesh,
        in_specs=(
            P("section", "shard", None, None, None),
            P(),
            P(),
            P(),
            P("section", None),
            P("section", None, "shard"),
            P("section", None, "shard"),
            P("section", "shard", None),
            P("section", None, None, None, None, None, None),
            P(),
            P("section", None),
            P("section", None, None),
            P("section", None, None),
        ),
        out_specs=(
            P("section", "shard", None, None),
            P("section", "shard", None, None),
            P("section", None, "shard", None),
        ),
        check_vma=False,
    )
```
